32 devices in a mesh: island: 8 (over y, x, core), fsdp: 4 (over z).
Axes of the slice: x: 2, y: 2, z: 4, core: 2. Of those that a mesh axis runs over, the one named last changes fastest.
Arguments:
- hidden: bfloat16 [4096, 4096], P(('island', 'fsdp')), may hold values from -6 to 6
- query_rows: bfloat16 [4096, 4096], P(('island', 'fsdp')), may hold values from -150 to 150
- key_rows: bfloat16 [4096, 512], P(('island', 'fsdp')), may hold values from -6 to 6
- targets: bfloat16 [4096, 4096], P(('island', 'fsdp')), may hold values from -6 to 6
- segment_ids: int32 [32, 128], P(('island', 'fsdp')), may hold values from 0 to 3, never falling along the last dimension, each value on 1 to 48 neighbouring positions
- first_moment: float32 [8, 4096, 512], P('island', 'fsdp'), may hold values from -0.0041432036 to 0.0041432036
- second_moment: float32 [8, 4096, 512], P('island', 'fsdp'), may hold values from 2.3841858e-07 to 3.8146973e-06
- anchor: float32 [4096, 512], P('fsdp', 'island'), may hold values from -6 to 6
- outer_momentum: float32 [4096, 512], P('fsdp', 'island'), may hold values from -0.3 to 0.3
- token_counts: int32 [8], P('island'), may hold values from 4096 to 12287
Outputs:
- new_anchor: float32 [4096, 512], P('fsdp', 'island')
- new_momentum: float32 [4096, 512], P('fsdp', 'island')
The draws below stay inside these ranges and needn't reach their ends.
Inputs may be any that keep to these rules, and one draw needn't show every extreme that they name: `segment_ids`: each row is one sequence: document numbers from 0 that never fall, each document 1 to 48 tokens, one of exactly 48.
All inputs are finite; a program needn't handle non-finite values.
Results may differ from the reference program's by a relative error of at most 0.004.
Values may be sent and summed in bfloat16 or wider, within the bound.
A program may use at most 64 MiB of HBM per device.

```python
import math
import jax
import jax.numpy as jnp
import numpy as np
from jax import lax

D = 4096
KVH = 4
QPK = 8
HD = 128
TOK_DEV = 128
DOCS = 4
DOC_MOST = 48
SEQS = 32
TOKENS = 4096
N_ISLAND = 8
N_FSDP = 4


def base_keys(key):
    drawn = jnp.clip(jax.random.normal(jax.random.fold_in(key, 11), (TOKENS, KVH, HD), jnp.float32), -5.0, 5.0)
    return drawn


def draw_key_rows(key, part):
    return base_keys(key).reshape(TOKENS, KVH * HD).astype(jnp.bfloat16)


def draw_query_rows(key, part):
    drawn = jnp.clip(jax.random.normal(jax.random.fold_in(key, 13), (TOKENS, KVH, QPK, HD), jnp.float32), -5.0, 5.0)
    return drawn.reshape(TOKENS, KVH * QPK * HD).astype(jnp.bfloat16)


def set_ends(values, rng, low, top_value):
    dims = values.shape
    spot = [jax.random.randint(jax.random.fold_in(rng, axis), (), 0, dims[axis]) for axis in range(len(dims))]
    values = values.at[tuple(spot)].set(low)
    longest = dims.index(max(dims))
    spot[longest] = (spot[longest] + 1) % dims[longest]
    return values.at[tuple(spot)].set(top_value)


def levels(rng, dims, split, least, largest):
    gain = 1.0
    for dim, blocks in split:
        draws = jax.random.uniform(jax.random.fold_in(jax.random.fold_in(rng, 6), dim), (blocks,), jnp.float32, least / len(split), largest / len(split))
        gain = gain * jnp.repeat(jnp.exp(draws), dims[dim] // blocks).reshape((-1,) + (1,) * (len(dims) - 1 - dim))
    return gain


def profile(number_of, total, most, lean):
    portions = [(1 << 20) // math.isqrt(rank ** lean) + 1 for rank in range(2, number_of + 1)]
    surplus, given = total - most - (number_of - 1), [1] * (number_of - 1)
    while surplus > 0:
        movable = [i for i in range(number_of - 1) if given[i] < most]
        pool, left = sum([portions[i] for i in movable]), surplus
        for i in movable:
            extra = min(most - given[i], max(1, left * portions[i] // pool), surplus)
            given[i] = given[i] + extra
            surplus = surplus - extra
    return np.array([most] + given)


def ragged_sizes(stream_key, amount, total, reach, slope):
    if amount == 2:
        one = jax.random.randint(stream_key, (), max(1, total - reach), min(reach, total - 1) + 1)
        return jnp.stack([one, total - one])
    tallies = jnp.asarray(profile(amount, total, reach, slope), jnp.int32)
    pairs = (amount - 1) // 2
    donor, taker = tallies[1:1 + 2 * pairs:2], tallies[2:2 + 2 * pairs:2]
    room = jnp.minimum(donor - 1, reach - taker)
    shifted = jax.random.randint(jax.random.fold_in(stream_key, 1), (pairs,), 0, 1 << 20) % (room + 1)
    tallies = tallies.at[1:1 + 2 * pairs:2].set(donor - shifted).at[2:2 + 2 * pairs:2].set(taker + shifted)
    return tallies[jax.random.permutation(jax.random.fold_in(stream_key, 2), amount)]


def centred(key, shape, spread, reach, cuts=(), held_as=jnp.bfloat16):
    array = jax.random.normal(key, shape, jnp.float32) * spread
    if len(cuts) > 0:
        array = levels(key, shape, cuts, -0.22, 0.18) * array
    return jnp.clip(array, min=-reach, max=reach).astype(held_as)


def setup_inputs(seed: int = 0) -> dict:
    arg_keys = jax.random.split(jax.random.key(seed), 11)
    return {
        "hidden": centred(arg_keys[0], (TOKENS, D), 1.0, 6.0, ((0, 32),)),
        "query_rows": draw_query_rows(jax.random.fold_in(arg_keys[10], 71), 0),
        "key_rows": draw_key_rows(jax.random.fold_in(arg_keys[10], 71), 0),
        "targets": centred(arg_keys[3], (TOKENS, KVH * QPK * HD), 1.0, 6.0, ((0, 32),)),
        "segment_ids": jax.vmap(lambda own: jnp.searchsorted(jnp.cumsum(ragged_sizes(own, DOCS, TOK_DEV, DOC_MOST, 0)), jnp.arange(TOK_DEV), side="right"))(jax.random.split(arg_keys[4], SEQS)).reshape((SEQS, TOK_DEV)).astype(jnp.int32),
        "first_moment": centred(arg_keys[5], (N_ISLAND, D, KVH * HD), (1.0 / (D * TOK_DEV * N_FSDP) ** 0.5), 0.0041432036, ((0, 8), (1, 4)), jnp.float32),
        "second_moment": jnp.clip(jnp.exp(math.log(3.814697265625e-06) - 2.7725887 * jax.random.uniform(arg_keys[6], (N_ISLAND, D, KVH * HD), jnp.float32) ** levels(arg_keys[6], (N_ISLAND, D, KVH * HD), ((0, 8), (1, 4)), -0.2, 0.2)), 2.384185791015625e-07, 3.814697265625e-06),
        "anchor": centred(arg_keys[7], (D, KVH * HD), 1.0, 6.0, ((0, 4), (1, 8)), jnp.float32),
        "outer_momentum": centred(arg_keys[8], (D, KVH * HD), 0.05, 0.3, ((0, 4), (1, 8)), jnp.float32),
        "token_counts": set_ends(jax.random.randint(arg_keys[9], (N_ISLAND,), 4096, 12288), jax.random.fold_in(arg_keys[9], 1), 4096, 12287).astype(jnp.int32),
    }


beta_one = 0.9
beta_two = 0.95
inner_rate = 0.05
decay = 0.1
epsilon = 1e-08
outer_rate = 0.7
outer_beta = 0.9

def attention_weights(query_rows, key_rows, segments):
    count = segments.shape[0]
    length = segments.shape[1]
    queries = query_rows.astype(jnp.float32).reshape(count, length, KVH, QPK, HD)
    keyed = key_rows.astype(jnp.float32).reshape(count, length, KVH, HD)
    scores = jnp.einsum('btgjd,bsgd->bgjts', queries, keyed) * (1.0 / math.sqrt(HD))
    place = jnp.arange(length)
    causal = place[None, :] <= place[:, None]
    same = segments[:, :, None] == segments[:, None, :]
    allowed = (causal[None] & same)[:, None, None]
    scores = jnp.where(allowed, scores, -jnp.inf)
    highest = lax.optimization_barrier(jnp.max(scores, axis=-1, keepdims=True))
    expo = jnp.exp(scores - highest)
    return (expo / lax.optimization_barrier(jnp.sum(expo, axis=-1, keepdims=True))).astype(jnp.bfloat16)

def reference(hidden, query_rows, key_rows, targets, segment_ids, first_moment, second_moment, anchor, outer_momentum, token_counts):
    group_rows = N_FSDP * TOK_DEV
    scale_in = 1.0 / math.sqrt(D)
    width = KVH * HD
    block = D // N_FSDP

    def island_delta(inputs):
        local_hidden, local_queries, local_keys, local_targets, segments, first, second = inputs
        attention = attention_weights(local_queries, local_keys, segments).astype(jnp.float32)
        hidden_blocks = local_hidden.astype(jnp.float32).reshape(group_rows, N_FSDP, block)
        weight = anchor
        for inner_step in range(2):
            rounded = lax.optimization_barrier(weight.astype(jnp.bfloat16)).astype(jnp.float32)
            blocks = jnp.einsum('rnc,ncw->nrw', hidden_blocks, rounded.reshape(N_FSDP, block, width))
            block_values = lax.optimization_barrier(blocks.astype(jnp.bfloat16)).astype(jnp.float32)
            values = (lax.optimization_barrier(jnp.sum(block_values, axis=0)) * scale_in).astype(jnp.bfloat16)
            mixed = jnp.einsum('bgjts,bsgd->btgjd', attention, values.astype(jnp.float32).reshape(N_FSDP, TOK_DEV, KVH, HD))
            error = ((mixed.reshape(group_rows, KVH * QPK * HD) - local_targets.astype(jnp.float32)) / group_rows).astype(jnp.bfloat16)
            back = jnp.einsum('bgjts,btgjd->bsgd', attention, error.astype(jnp.float32).reshape(N_FSDP, TOK_DEV, KVH, QPK, HD))
            value_grad = (back.reshape(group_rows, width) * scale_in).astype(jnp.bfloat16)
            grad = jnp.dot(local_hidden.T, value_grad, preferred_element_type=jnp.float32)
            first = beta_one * first + (1.0 - beta_one) * grad
            second = beta_two * second + (1.0 - beta_two) * grad * grad
            weight = weight - inner_rate * (first / (jnp.sqrt(second) + epsilon) + decay * weight)
        return anchor - weight
    deltas = lax.map(island_delta, (hidden.reshape(N_ISLAND, group_rows, D), query_rows.reshape(N_ISLAND, group_rows, KVH * QPK * HD), key_rows.reshape(N_ISLAND, group_rows, width), targets.reshape(N_ISLAND, group_rows, KVH * QPK * HD), segment_ids.reshape(N_ISLAND, N_FSDP, TOK_DEV), first_moment, second_moment))
    counts = token_counts.astype(jnp.float32)
    average = lax.optimization_barrier(jnp.sum(counts[:, None, None] * deltas, axis=0)) / jnp.sum(counts)
    new_momentum = outer_beta * outer_momentum + average
    new_anchor = anchor - outer_rate * (average + outer_beta * new_momentum)
    return (new_anchor, new_momentum)
```

```python
import functools
import math

import jax
import jax.numpy as jnp
from jax import lax
from jax.experimental import pallas as pl
from jax.experimental.pallas import tpu as pltpu
from jax.sharding import PartitionSpec as P

KVH = 4
QPK = 8
HD = 128


beta_one = 0.9
beta_two = 0.95
inner_rate = 0.05
decay = 0.1
epsilon = 1e-08
outer_rate = 0.7
outer_beta = 0.9


def attention_weights(query_rows, key_rows, segments):
    length = segments.shape[0]
    queries = query_rows.reshape(length, KVH, QPK, HD)
    keyed = key_rows.reshape(length, KVH, HD)
    scores = jnp.einsum("tgjd,sgd->gjts", queries, keyed, preferred_element_type=jnp.float32) * (
        1.0 / math.sqrt(HD)
    )
    place = jnp.arange(length)
    allowed = (place[None, :] <= place[:, None]) & (segments[:, None] == segments[None, :])
    scores = jnp.where(allowed[None, None], scores, -jnp.inf)
    highest = jnp.max(scores, axis=-1, keepdims=True)
    expo = jnp.exp(scores - highest)
    return (expo / jnp.sum(expo, axis=-1, keepdims=True)).astype(jnp.bfloat16)


def on_device(
    hidden,
    query_rows,
    key_rows,
    targets,
    segment_ids,
    first_moment,
    second_moment,
    anchor,
    outer_momentum,
    token_counts,
):
    rows = hidden.shape[0]
    width = key_rows.shape[1]
    group_rows = rows * lax.axis_size("fsdp")
    scale_in = 1.0 / math.sqrt(hidden.shape[1])
    attention = attention_weights(query_rows, key_rows, segment_ids[0])
    master = lax.all_gather(anchor, "island", axis=1, tiled=True)
    start_point = master
    block = master.shape[0]
    first = first_moment[0]
    second = second_moment[0]
    feature_rows = lax.all_to_all(hidden, "fsdp", split_axis=1, concat_axis=0, tiled=True)
    for inner_step in range(2):
        sent_rows = master.astype(jnp.bfloat16)
        blocks = jnp.dot(feature_rows, sent_rows, preferred_element_type=jnp.float32)
        pieces = lax.all_to_all(
            blocks.astype(jnp.bfloat16), "fsdp", split_axis=0, concat_axis=0, tiled=True
        )
        projected = jnp.sum(pieces.reshape(-1, rows, width).astype(jnp.float32), axis=0)
        values = (projected * scale_in).astype(jnp.bfloat16)
        mixed = jnp.einsum(
            "gjts,sgd->tgjd",
            attention,
            values.reshape(rows, KVH, HD),
            preferred_element_type=jnp.float32,
        )
        error = (
            (mixed.reshape(rows, KVH * QPK * HD) - targets.astype(jnp.float32)) / group_rows
        ).astype(jnp.bfloat16)
        back = jnp.einsum(
            "gjts,tgjd->sgd",
            attention,
            error.reshape(rows, KVH, QPK, HD),
            preferred_element_type=jnp.float32,
        )
        value_grad = (back.reshape(rows, width) * scale_in).astype(jnp.bfloat16)
        grad = lax.dot_general(
            feature_rows,
            lax.all_gather(value_grad, "fsdp", axis=0, tiled=True),
            (((0,), (0,)), ((), ())),
            preferred_element_type=jnp.float32,
        )
        first = beta_one * first + (1.0 - beta_one) * grad
        second = beta_two * second + (1.0 - beta_two) * grad * grad
        master = master - inner_rate * (first / (jnp.sqrt(second) + epsilon) + decay * master)
    delta = start_point - master
    groups = lax.axis_size("island")
    own_count = token_counts[0].astype(jnp.float32)
    total_count = lax.psum(own_count, "island")
    received = lax.all_to_all(
        own_count / total_count * delta, "island", split_axis=1, concat_axis=0, tiled=True
    )
    average = jnp.sum(received.reshape(groups, block, anchor.shape[1]), axis=0)
    new_momentum = outer_beta * outer_momentum + average
    new_anchor = anchor - outer_rate * (average + outer_beta * new_momentum)
    return (new_anchor, new_momentum)


MESH = pl.DeviceIdType.MESH
BF = jnp.bfloat16
F32 = jnp.float32


def dot(left, right):
    return jnp.dot(left, right, preferred_element_type=F32)


def round_kernel(
    ni,
    nf,
    hidden,
    query,
    keys,
    targets,
    segments,
    first_in,
    second_in,
    anchor,
    momentum,
    counts,
    new_anchor,
    new_momentum,
    q_buf,
    t_buf,
    first,
    second,
    feat,
    feat_t,
    att,
    att_t,
    weight,
    master,
    delta,
    a_buf,
    bv_send,
    bv_recv,
    vg_buf,
    d_send,
    d_recv,
    local_sem,
    h_send_sem,
    h_recv_sem,
    a_send_sem,
    a_recv_sem,
    b_send_sem,
    b_recv_sem,
    v_send_sem,
    v_recv_sem,
    d_send_sem,
    d_recv_sem,
):
    me = lax.axis_index("fsdp")
    island = lax.axis_index("island")
    rows = feat.shape[1]
    block = feat.shape[2]
    half = block // 2
    group_rows = rows * nf
    scale_in = 1.0 / math.sqrt(hidden.shape[1])

    def ahead(step):
        return lax.rem(me + step, nf)

    def behind(step):
        return lax.rem(me + nf - step, nf)

    def peer(step):
        return lax.rem(island + step, ni)

    loads = [
        pltpu.make_async_copy(
            hidden.at[:, pl.ds(pl.multiple_of(me * block, block), block)],
            feat.at[0],
            local_sem.at[0],
        ),
        pltpu.make_async_copy(query, q_buf, local_sem.at[1]),
        pltpu.make_async_copy(targets, t_buf, local_sem.at[2]),
        pltpu.make_async_copy(first_in, first, local_sem.at[3]),
        pltpu.make_async_copy(second_in, second, local_sem.at[4]),
    ]
    for load in loads:
        load.start()

    barrier = pltpu.get_barrier_semaphore()
    for step in range(1, nf):
        pl.semaphore_signal(
            barrier, inc=1, device_id=(island, ahead(step)), device_id_type=MESH
        )
    for step in range(1, ni):
        pl.semaphore_signal(barrier, inc=1, device_id=(peer(step), me), device_id_type=MESH)

    wide = anchor[...].astype(F32)
    packed = jnp.concatenate([wide[:half], wide[half:]], axis=1)
    a_buf[island, 0:half] = packed.astype(BF)
    count = counts[0]
    high = (count // 256).astype(F32)
    low = (count % 256).astype(F32)
    upper = lax.broadcasted_iota(jnp.int32, (16, 128), 0) < 8
    a_buf[island, half : half + 16] = jnp.where(upper, high, low).astype(BF)

    pl.semaphore_wait(barrier, ni + nf - 2)

    def send_hidden(step):
        return pltpu.make_async_remote_copy(
            src_ref=hidden.at[:, pl.ds(pl.multiple_of(ahead(step) * block, block), block)],
            dst_ref=feat.at[step],
            send_sem=h_send_sem.at[step],
            recv_sem=h_recv_sem.at[step],
            device_id=(island, ahead(step)),
            device_id_type=MESH,
        )

    def send_anchor(step):
        return pltpu.make_async_remote_copy(
            src_ref=a_buf.at[island],
            dst_ref=a_buf.at[island],
            send_sem=a_send_sem.at[step],
            recv_sem=a_recv_sem.at[island],
            device_id=(peer(step), me),
            device_id_type=MESH,
        )

    def await_anchor(step):
        owner = peer(step)
        return pltpu.make_async_remote_copy(
            src_ref=a_buf.at[owner],
            dst_ref=a_buf.at[owner],
            send_sem=a_send_sem.at[step],
            recv_sem=a_recv_sem.at[owner],
            device_id=(peer(step), me),
            device_id_type=MESH,
        )

    def send_block(turn, head, step):
        return pltpu.make_async_remote_copy(
            src_ref=bv_send.at[turn, head, step],
            dst_ref=bv_recv.at[turn, head, step],
            send_sem=b_send_sem.at[turn, head, step],
            recv_sem=b_recv_sem.at[turn, head, step],
            device_id=(island, behind(step)),
            device_id_type=MESH,
        )

    def send_grad(turn, head, step):
        return pltpu.make_async_remote_copy(
            src_ref=vg_buf.at[turn, head, 0:rows],
            dst_ref=vg_buf.at[turn, head, step * rows : (step + 1) * rows],
            send_sem=v_send_sem.at[turn, head, step],
            recv_sem=v_recv_sem.at[turn, head, step],
            device_id=(island, ahead(step)),
            device_id_type=MESH,
        )

    def send_delta(owner):
        return pltpu.make_async_remote_copy(
            src_ref=d_send.at[owner],
            dst_ref=d_recv.at[island],
            send_sem=d_send_sem.at[owner],
            recv_sem=d_recv_sem.at[island],
            device_id=(owner, me),
            device_id_type=MESH,
        )

    def await_delta(step):
        owner = peer(step)
        return pltpu.make_async_remote_copy(
            src_ref=d_send.at[owner],
            dst_ref=d_recv.at[owner],
            send_sem=d_send_sem.at[owner],
            recv_sem=d_recv_sem.at[owner],
            device_id=(owner, me),
            device_id_type=MESH,
        )

    near_first = [1, 3, 2] if nf == 4 else list(range(1, nf))
    for step in near_first:
        send_hidden(step).start()
    for step in range(1, ni):
        send_anchor(step).start()

    loads[1].wait()
    seg = jnp.broadcast_to(segments[...].astype(F32), (rows, rows))
    place_t = lax.broadcasted_iota(jnp.int32, (rows, rows), 0)
    place_s = lax.broadcasted_iota(jnp.int32, (rows, rows), 1)
    allowed = (place_s <= place_t) & (seg == seg.T)

    def attend(number, carry):
        head = number // QPK
        within = number % QPK
        queries = q_buf[:, pl.ds(pl.multiple_of(number * HD, HD), HD)]
        keyed = keys[:, pl.ds(pl.multiple_of(head * HD, HD), HD)]
        scores = lax.dot_general(
            queries, keyed, (((1,), (1,)), ((), ())), preferred_element_type=F32
        ) * (1.0 / math.sqrt(HD))
        scores = jnp.where(allowed, scores, -1e30)
        expo = jnp.exp(scores - jnp.max(scores, axis=1, keepdims=True))
        ratio = expo / jnp.sum(expo, axis=1, keepdims=True)
        at = pl.ds(pl.multiple_of(within * rows, rows), rows)
        att[head, at, :] = ratio.astype(BF)
        att_t[head, :, at] = ratio.T.astype(BF)
        return carry

    lax.fori_loop(0, KVH * QPK, attend, 0, unroll=2)

    for step in range(1, ni):
        await_anchor(step).wait_recv()
    left = lax.broadcasted_iota(jnp.int32, (half, 128), 1) < 64

    def merge(head, carry):
        even = a_buf[2 * head, 0:half].astype(F32)
        odd = a_buf[2 * head + 1, 0:half].astype(F32)
        top = jnp.where(left, even, pltpu.roll(odd, 64, 1))
        bottom = jnp.where(left, pltpu.roll(even, 64, 1), odd)
        master[head, 0:half] = top
        master[head, half:block] = bottom
        weight[head, 0:half] = top.astype(BF)
        weight[head, half:block] = bottom.astype(BF)
        return carry

    lax.fori_loop(0, KVH, merge, 0)

    for step in [0] + near_first:
        if step == 0:
            loads[0].wait()
        else:
            send_hidden(step).wait_recv()

        def first_blocks(head, carry, step=step):
            piece = dot(feat[step], weight[head]).astype(BF)
            if step == 0:
                bv_recv[0, head, 0] = piece
            else:
                bv_send[0, head, step] = piece
                send_block(0, head, step).start()
            return carry

        lax.fori_loop(0, KVH, first_blocks, 0)
    for step in range(nf):
        feat_t[:, step * rows : (step + 1) * rows] = feat[step].T

    def attention_turn(turn, head):
        for step in range(1, nf):
            send_block(turn, head, step).wait_recv()
        projected = bv_recv[turn, head, 0].astype(F32)
        for step in range(1, nf):
            projected = projected + bv_recv[turn, head, step].astype(F32)
        values = (projected * scale_in).astype(BF)
        back = jnp.zeros((rows, HD), F32)
        for within in range(QPK):
            lot = slice(within * rows, (within + 1) * rows)
            mixed = dot(att[head, lot, :], values)
            aim = t_buf[:, pl.ds(pl.multiple_of((head * QPK + within) * HD, HD), HD)]
            error = ((mixed - aim.astype(F32)) * (1.0 / group_rows)).astype(BF)
            back = back + dot(att_t[head, :, lot], error)
        vg_buf[turn, head, 0:rows] = (back * scale_in).astype(BF)
        for step in near_first:
            send_grad(turn, head, step).start()

    def update_turn(turn, head):
        for step in range(1, nf):
            send_grad(turn, head, step).wait_recv()
        lanes = pl.ds(pl.multiple_of(head * HD, HD), HD)
        part = block // 4

        def rows_part(index, carry):
            at = pl.ds(pl.multiple_of(index * part, part), part)
            grad = dot(feat_t[at, :], vg_buf[turn, head])
            one = beta_one * first[0, at, lanes] + (1.0 - beta_one) * grad
            two = beta_two * second[0, at, lanes] + (1.0 - beta_two) * grad * grad
            now = master[head, at]
            move = inner_rate * (one / (jnp.sqrt(two) + epsilon) + decay * now)
            if turn == 0:
                first[0, at, lanes] = one
                second[0, at, lanes] = two
                delta[head, at] = move
                later = now - move
                master[head, at] = later
                weight[head, at] = later.astype(BF)
            else:
                delta[head, at] = (delta[head, at] + move) * count.astype(F32)
            return carry

        lax.fori_loop(0, 4, rows_part, 0)

    def turn_one_attention(head, carry):
        attention_turn(0, head)
        return carry

    def turn_one_update(head, carry):
        update_turn(0, head)
        for step in [1, 3, 2, 0] if nf == 4 else list(range(nf)):
            piece = dot(feat[step], weight[head]).astype(BF)
            if step == 0:
                bv_recv[1, head, 0] = piece
            else:
                bv_send[1, head, step] = piece
                send_block(1, head, step).start()
        return carry

    def turn_two_attention(head, carry):
        attention_turn(1, head)
        return carry

    def turn_two_update(head, carry):
        update_turn(1, head)
        top = delta[head, 0:half]
        bottom = delta[head, half:block]
        d_send[2 * head] = jnp.where(left, top, pltpu.roll(bottom, 64, 1)).astype(BF)
        d_send[2 * head + 1] = jnp.where(left, pltpu.roll(top, 64, 1), bottom).astype(BF)
        for odd in range(2):
            owner = 2 * head + odd

            @pl.when(owner != island)
            def _():
                send_delta(owner).start()

        return carry

    loads[2].wait()
    lax.fori_loop(0, KVH, turn_one_attention, 0)
    loads[3].wait()
    loads[4].wait()
    lax.fori_loop(0, KVH, turn_one_update, 0)
    lax.fori_loop(0, KVH, turn_two_attention, 0)
    lax.fori_loop(0, KVH, turn_two_update, 0)

    for step in range(1, ni):
        await_delta(step).wait_recv()
    total = d_send[island].astype(F32)
    for step in range(1, ni):
        total = total + d_recv[peer(step)].astype(F32)
    tally = jnp.zeros((16, 128), F32)
    for owner in range(ni):
        tally = tally + a_buf[owner, half : half + 16].astype(F32)
    whole = tally[0:1] * 256.0 + tally[8:9]
    average = total / whole
    pieces = (average[:, :64], pltpu.roll(average, 64, 1)[:, :64])
    for place in range(2):
        lot = slice(place * half, (place + 1) * half)
        fresh = outer_beta * momentum[lot] + pieces[place]
        new_momentum[lot] = fresh
        new_anchor[lot] = anchor[lot] - outer_rate * (pieces[place] + outer_beta * fresh)

    for step in range(1, nf):
        send_hidden(step).wait_send()
    for step in range(1, ni):
        send_anchor(step).wait_send()
        await_delta(step).wait_send()

    def drain(number, carry):
        turn = number // KVH
        head = number % KVH
        for step in range(1, nf):
            send_block(turn, head, step).wait_send()
            send_grad(turn, head, step).wait_send()
        return carry

    lax.fori_loop(0, 2 * KVH, drain, 0)


def on_device_any(*args):
    hidden, query, keys, _, _, first, _, anchor, _, _ = args
    ni = lax.axis_size("island")
    nf = lax.axis_size("fsdp")
    rows = hidden.shape[0]
    block, columns = anchor.shape
    if (rows, columns, ni, block) != (HD, HD // 2, 2 * KVH, 8 * HD):
        return on_device(*args)
    vmem = pl.BlockSpec(memory_space=pltpu.VMEM)
    anywhere = pl.BlockSpec(memory_space=pl.ANY)
    dma = pltpu.SemaphoreType.DMA
    return pl.pallas_call(
        functools.partial(round_kernel, ni, nf),
        out_shape=[jax.ShapeDtypeStruct(anchor.shape, F32)] * 2,
        in_specs=[
            anywhere,
            anywhere,
            vmem,
            anywhere,
            vmem,
            anywhere,
            anywhere,
            vmem,
            vmem,
            pl.BlockSpec(memory_space=pltpu.SMEM),
        ],
        out_specs=[vmem, vmem],
        scratch_shapes=[
            pltpu.VMEM(query.shape, BF),
            pltpu.VMEM(query.shape, BF),
            pltpu.VMEM(first.shape, F32),
            pltpu.VMEM(first.shape, F32),
            pltpu.VMEM((nf, rows, block), BF),
            pltpu.VMEM((block, nf * rows), BF),
            pltpu.VMEM((KVH, QPK * rows, rows), BF),
            pltpu.VMEM((KVH, rows, QPK * rows), BF),
            pltpu.VMEM((KVH, block, HD), BF),
            pltpu.VMEM((KVH, block, HD), F32),
            pltpu.VMEM((KVH, block, HD), F32),
            pltpu.VMEM((ni, block // 2 + 16, 128), BF),
            pltpu.VMEM((2, KVH, nf, rows, HD), BF),
            pltpu.VMEM((2, KVH, nf, rows, HD), BF),
            pltpu.VMEM((2, KVH, nf * rows, HD), BF),
            pltpu.VMEM((ni, block // 2, 128), BF),
            pltpu.VMEM((ni, block // 2, 128), BF),
            dma((5,)),
            dma((nf,)),
            dma((nf,)),
            dma((ni,)),
            dma((ni,)),
            dma((2, KVH, nf)),
            dma((2, KVH, nf)),
            dma((2, KVH, nf)),
            dma((2, KVH, nf)),
            dma((ni,)),
            dma((ni,)),
        ],
        compiler_params=pltpu.CompilerParams(
            collective_id=0, has_side_effects=True, vmem_limit_bytes=44 * 2**20
        ),
    )(*args)


def solution(mesh):
    in_specs = (
        P(("island", "fsdp"), None),
        P(("island", "fsdp"), None),
        P(("island", "fsdp"), None),
        P(("island", "fsdp"), None),
        P(("island", "fsdp"), None),
        P("island", "fsdp", None),
        P("island", "fsdp", None),
        P("fsdp", "island"),
        P("fsdp", "island"),
        P("island"),
    )
    out_specs = (P("fsdp", "island"), P("fsdp", "island"))
    return jax.shard_map(
        on_device_any, mesh=mesh, in_specs=in_specs, out_specs=out_specs, check_vma=False
    )
```

```python
import functools
import math

import jax
import jax.numpy as jnp
from jax import lax
from jax.experimental import pallas as pl
from jax.experimental.pallas import tpu as pltpu
from jax.sharding import PartitionSpec as P

KVH = 4
QPK = 8
HD = 128


beta_one = 0.9
beta_two = 0.95
inner_rate = 0.05
decay = 0.1
epsilon = 1e-08
outer_rate = 0.7
outer_beta = 0.9


def attention_weights(query_rows, key_rows, segments):
    length = segments.shape[0]
    queries = query_rows.reshape(length, KVH, QPK, HD)
    keyed = key_rows.reshape(length, KVH, HD)
    scores = jnp.einsum("tgjd,sgd->gjts", queries, keyed, preferred_element_type=jnp.float32) * (
        1.0 / math.sqrt(HD)
    )
    place = jnp.arange(length)
    allowed = (place[None, :] <= place[:, None]) & (segments[:, None] == segments[None, :])
    scores = jnp.where(allowed[None, None], scores, -jnp.inf)
    highest = jnp.max(scores, axis=-1, keepdims=True)
    expo = jnp.exp(scores - highest)
    return (expo / jnp.sum(expo, axis=-1, keepdims=True)).astype(jnp.bfloat16)


def on_device(
    hidden,
    query_rows,
    key_rows,
    targets,
    segment_ids,
    first_moment,
    second_moment,
    anchor,
    outer_momentum,
    token_counts,
):
    rows = hidden.shape[0]
    width = key_rows.shape[1]
    group_rows = rows * lax.axis_size("fsdp")
    scale_in = 1.0 / math.sqrt(hidden.shape[1])
    attention = attention_weights(query_rows, key_rows, segment_ids[0])
    master = lax.all_gather(anchor, "island", axis=1, tiled=True)
    start_point = master
    block = master.shape[0]
    first = first_moment[0]
    second = second_moment[0]
    feature_rows = lax.all_to_all(hidden, "fsdp", split_axis=1, concat_axis=0, tiled=True)
    for inner_step in range(2):
        sent_rows = master.astype(jnp.bfloat16)
        blocks = jnp.dot(feature_rows, sent_rows, preferred_element_type=jnp.float32)
        pieces = lax.all_to_all(
            blocks.astype(jnp.bfloat16), "fsdp", split_axis=0, concat_axis=0, tiled=True
        )
        projected = jnp.sum(pieces.reshape(-1, rows, width).astype(jnp.float32), axis=0)
        values = (projected * scale_in).astype(jnp.bfloat16)
        mixed = jnp.einsum(
            "gjts,sgd->tgjd",
            attention,
            values.reshape(rows, KVH, HD),
            preferred_element_type=jnp.float32,
        )
        error = (
            (mixed.reshape(rows, KVH * QPK * HD) - targets.astype(jnp.float32)) / group_rows
        ).astype(jnp.bfloat16)
        back = jnp.einsum(
            "gjts,tgjd->sgd",
            attention,
            error.reshape(rows, KVH, QPK, HD),
            preferred_element_type=jnp.float32,
        )
        value_grad = (back.reshape(rows, width) * scale_in).astype(jnp.bfloat16)
        grad = lax.dot_general(
            feature_rows,
            lax.all_gather(value_grad, "fsdp", axis=0, tiled=True),
            (((0,), (0,)), ((), ())),
            preferred_element_type=jnp.float32,
        )
        first = beta_one * first + (1.0 - beta_one) * grad
        second = beta_two * second + (1.0 - beta_two) * grad * grad
        master = master - inner_rate * (first / (jnp.sqrt(second) + epsilon) + decay * master)
    delta = start_point - master
    groups = lax.axis_size("island")
    own_count = token_counts[0].astype(jnp.float32)
    total_count = lax.psum(own_count, "island")
    received = lax.all_to_all(
        own_count / total_count * delta, "island", split_axis=1, concat_axis=0, tiled=True
    )
    average = jnp.sum(received.reshape(groups, block, anchor.shape[1]), axis=0)
    new_momentum = outer_beta * outer_momentum + average
    new_anchor = anchor - outer_rate * (average + outer_beta * new_momentum)
    return (new_anchor, new_momentum)


MESH = pl.DeviceIdType.MESH
BF = jnp.bfloat16
F32 = jnp.float32


def dot(left, right):
    return jnp.dot(left, right, preferred_element_type=F32)


def round_kernel(
    ni,
    nf,
    hidden,
    query,
    keys_in,
    targets,
    segments,
    first_in,
    second_in,
    anchor_in,
    momentum_in,
    counts,
    new_anchor,
    new_momentum,
    q_buf,
    t_buf,
    keys,
    anchor,
    momentum,
    first,
    second,
    feat,
    feat_t,
    att,
    att_t,
    weight,
    master,
    delta,
    a_buf,
    c_buf,
    bv_send,
    bv_recv,
    vg_buf,
    d_send,
    d_recv,
    local_sem,
    h_send_sem,
    h_recv_sem,
    a_send_sem,
    a_recv_sem,
    c_send_sem,
    c_recv_sem,
    b_send_sem,
    b_recv_sem,
    v_send_sem,
    v_recv_sem,
    d_send_sem,
    d_recv_sem,
):
    me = lax.axis_index("fsdp")
    island = lax.axis_index("island")
    rows = feat.shape[1]
    block = feat.shape[2]
    columns = anchor.shape[0]
    group_rows = rows * nf
    scale_in = 1.0 / math.sqrt(hidden.shape[1])

    def ahead(step):
        return lax.rem(me + step, nf)

    def behind(step):
        return lax.rem(me + nf - step, nf)

    def peer(step):
        return lax.rem(island + step, ni)

    loads = [
        pltpu.make_async_copy(anchor_in, anchor, local_sem.at[0]),
        pltpu.make_async_copy(query, q_buf, local_sem.at[1]),
        pltpu.make_async_copy(targets, t_buf, local_sem.at[2]),
        pltpu.make_async_copy(first_in, first, local_sem.at[3]),
        pltpu.make_async_copy(second_in, second, local_sem.at[4]),
        pltpu.make_async_copy(keys_in, keys, local_sem.at[5]),
        pltpu.make_async_copy(momentum_in, momentum, local_sem.at[6]),
        pltpu.make_async_copy(
            hidden.at[:, pl.ds(pl.multiple_of(me * block, block), block)],
            feat.at[0],
            local_sem.at[7],
        ),
    ]
    for number in (0, 5, 1):
        loads[number].start()

    barrier = pltpu.get_barrier_semaphore()
    for step in range(1, nf):
        pl.semaphore_signal(
            barrier, inc=1, device_id=(island, ahead(step)), device_id_type=MESH
        )
    for step in range(1, ni):
        pl.semaphore_signal(barrier, inc=1, device_id=(peer(step), me), device_id_type=MESH)

    pl.semaphore_wait(barrier, ni + nf - 2)

    def send_hidden(step):
        return pltpu.make_async_remote_copy(
            src_ref=hidden.at[:, pl.ds(pl.multiple_of(ahead(step) * block, block), block)],
            dst_ref=feat.at[step],
            send_sem=h_send_sem.at[step],
            recv_sem=h_recv_sem.at[step],
            device_id=(island, ahead(step)),
            device_id_type=MESH,
        )

    def send_anchor(step):
        return pltpu.make_async_remote_copy(
            src_ref=a_buf.at[island],
            dst_ref=a_buf.at[island],
            send_sem=a_send_sem.at[step],
            recv_sem=a_recv_sem.at[island],
            device_id=(peer(step), me),
            device_id_type=MESH,
        )

    def await_anchor(step):
        owner = peer(step)
        return pltpu.make_async_remote_copy(
            src_ref=a_buf.at[owner],
            dst_ref=a_buf.at[owner],
            send_sem=a_send_sem.at[step],
            recv_sem=a_recv_sem.at[owner],
            device_id=(peer(step), me),
            device_id_type=MESH,
        )

    def send_count(step):
        return pltpu.make_async_remote_copy(
            src_ref=c_buf.at[island],
            dst_ref=c_buf.at[island],
            send_sem=c_send_sem.at[step],
            recv_sem=c_recv_sem.at[island],
            device_id=(peer(step), me),
            device_id_type=MESH,
        )

    def await_count(step):
        owner = peer(step)
        return pltpu.make_async_remote_copy(
            src_ref=c_buf.at[owner],
            dst_ref=c_buf.at[owner],
            send_sem=c_send_sem.at[step],
            recv_sem=c_recv_sem.at[owner],
            device_id=(owner, me),
            device_id_type=MESH,
        )

    def order(number):
        return lax.rem(number + island // 2, KVH)

    def send_block(turn, head, step):
        return pltpu.make_async_remote_copy(
            src_ref=bv_send.at[turn, head, step],
            dst_ref=bv_recv.at[turn, head, step],
            send_sem=b_send_sem.at[turn, head, step],
            recv_sem=b_recv_sem.at[turn, head, step],
            device_id=(island, behind(step)),
            device_id_type=MESH,
        )

    def send_grad(turn, head, step):
        return pltpu.make_async_remote_copy(
            src_ref=vg_buf.at[turn, head, 0:rows],
            dst_ref=vg_buf.at[turn, head, step * rows : (step + 1) * rows],
            send_sem=v_send_sem.at[turn, head, step],
            recv_sem=v_recv_sem.at[turn, head, step],
            device_id=(island, ahead(step)),
            device_id_type=MESH,
        )

    def send_delta(owner):
        return pltpu.make_async_remote_copy(
            src_ref=d_send.at[owner],
            dst_ref=d_recv.at[island],
            send_sem=d_send_sem.at[owner],
            recv_sem=d_recv_sem.at[island],
            device_id=(owner, me),
            device_id_type=MESH,
        )

    def await_delta(step):
        owner = peer(step)
        return pltpu.make_async_remote_copy(
            src_ref=d_send.at[owner],
            dst_ref=d_recv.at[owner],
            send_sem=d_send_sem.at[owner],
            recv_sem=d_recv_sem.at[owner],
            device_id=(owner, me),
            device_id_type=MESH,
        )

    near_first = [1, 3, 2] if nf == 4 else list(range(1, nf))
    for step in near_first:
        send_hidden(step).start()
    loads[0].wait()
    a_buf[island] = anchor[...].astype(BF)
    count = counts[0]
    high = (count // 256).astype(F32)
    low = (count % 256).astype(F32)
    upper = lax.broadcasted_iota(jnp.int32, (16, 128), 0) < 8
    c_buf[island] = jnp.where(upper, high, low).astype(BF)
    for step in range(1, ni):
        send_anchor(step).start()
        send_count(step).start()
    for number in (7, 2, 3, 4, 6):
        loads[number].start()

    loads[5].wait()
    loads[1].wait()
    seg = jnp.broadcast_to(segments[...].astype(F32), (rows, rows))
    place_t = lax.broadcasted_iota(jnp.int32, (rows, rows), 0)
    place_s = lax.broadcasted_iota(jnp.int32, (rows, rows), 1)
    allowed = (place_s <= place_t) & (seg == seg.T)

    def attend(number, carry):
        head = number // QPK
        within = number % QPK
        queries = q_buf[:, pl.ds(pl.multiple_of(number * HD, HD), HD)]
        keyed = keys[:, pl.ds(pl.multiple_of(head * HD, HD), HD)]
        scores = lax.dot_general(
            queries, keyed, (((1,), (1,)), ((), ())), preferred_element_type=F32
        ) * (1.0 / math.sqrt(HD))
        scores = jnp.where(allowed, scores, -1e30)
        expo = jnp.exp(scores - jnp.max(scores, axis=1, keepdims=True))
        ratio = expo / jnp.sum(expo, axis=1, keepdims=True)
        at = pl.ds(pl.multiple_of(within * rows, rows), rows)
        att[head, at, :] = ratio.astype(BF)
        att_t[head, :, at] = ratio.T.astype(BF)
        return carry

    lax.fori_loop(0, KVH * QPK, attend, 0, unroll=2)

    for step in range(1, ni):
        await_anchor(step).wait_recv()

    def merge(head, carry):
        both = jnp.concatenate([a_buf[2 * head], a_buf[2 * head + 1]], axis=0).T
        weight[head] = both
        master[head] = both.astype(F32)
        return carry

    lax.fori_loop(0, KVH, merge, 0)

    for step in [0] + near_first:
        if step == 0:
            loads[7].wait()
        else:
            send_hidden(step).wait_recv()

        def first_blocks(number, carry, step=step):
            head = order(number)
            piece = dot(feat[step], weight[head]).astype(BF)
            if step == 0:
                bv_recv[0, head, 0] = piece
            else:
                bv_send[0, head, step] = piece
                send_block(0, head, step).start()
            return carry

        lax.fori_loop(0, KVH, first_blocks, 0)
    for step in range(nf):
        feat_t[:, step * rows : (step + 1) * rows] = feat[step].T

    def attention_turn(turn, head):
        for step in range(1, nf):
            send_block(turn, head, step).wait_recv()
        projected = bv_recv[turn, head, 0].astype(F32)
        for step in range(1, nf):
            projected = projected + bv_recv[turn, head, step].astype(F32)
        values = (projected * scale_in).astype(BF)
        back = jnp.zeros((rows, HD), F32)
        for within in range(QPK):
            lot = slice(within * rows, (within + 1) * rows)
            mixed = dot(att[head, lot, :], values)
            aim = t_buf[:, pl.ds(pl.multiple_of((head * QPK + within) * HD, HD), HD)]
            error = ((mixed - aim.astype(F32)) * (1.0 / group_rows)).astype(BF)
            back = back + dot(att_t[head, :, lot], error)
        vg_buf[turn, head, 0:rows] = (back * scale_in).astype(BF)
        for step in near_first:
            send_grad(turn, head, step).start()

    def update_turn(turn, head):
        for step in range(1, nf):
            send_grad(turn, head, step).wait_recv()
        lanes = pl.ds(pl.multiple_of(head * HD, HD), HD)
        part = block // 4

        def rows_part(index, carry):
            at = pl.ds(pl.multiple_of(index * part, part), part)
            grad = dot(feat_t[at, :], vg_buf[turn, head])
            one = beta_one * first[0, at, lanes] + (1.0 - beta_one) * grad
            two = beta_two * second[0, at, lanes] + (1.0 - beta_two) * grad * grad
            now = master[head, at]
            move = inner_rate * (one / (jnp.sqrt(two) + epsilon) + decay * now)
            if turn == 0:
                first[0, at, lanes] = one
                second[0, at, lanes] = two
                delta[head, at] = move
                later = now - move
                master[head, at] = later
                weight[head, at] = later.astype(BF)
            else:
                delta[head, at] = (delta[head, at] + move) * count.astype(F32)
            return carry

        lax.fori_loop(0, 4, rows_part, 0)

    def turn_one_attention(number, carry):
        head = order(number)
        attention_turn(0, head)
        return carry

    def turn_one_update(number, carry):
        head = order(number)
        update_turn(0, head)
        for step in [1, 3, 2, 0] if nf == 4 else list(range(nf)):
            piece = dot(feat[step], weight[head]).astype(BF)
            if step == 0:
                bv_recv[1, head, 0] = piece
            else:
                bv_send[1, head, step] = piece
                send_block(1, head, step).start()
        return carry

    def turn_two_attention(number, carry):
        head = order(number)
        attention_turn(1, head)
        return carry

    def turn_two_update(number, carry):
        head = order(number)
        update_turn(1, head)
        turned = delta[head].astype(BF).T
        d_send[2 * head] = turned[:columns]
        d_send[2 * head + 1] = turned[columns:]
        for odd in range(2):
            owner = 2 * head + odd

            @pl.when(owner != island)
            def _():
                send_delta(owner).start()

        return carry

    loads[2].wait()
    lax.fori_loop(0, KVH, turn_one_attention, 0)
    loads[3].wait()
    loads[4].wait()
    lax.fori_loop(0, KVH, turn_one_update, 0)
    lax.fori_loop(0, KVH, turn_two_attention, 0)
    lax.fori_loop(0, KVH, turn_two_update, 0)

    for step in range(1, ni):
        await_delta(step).wait_recv()
    total = d_send[island].astype(F32)
    for step in range(1, ni):
        total = total + d_recv[peer(step)].astype(F32)
    tally = c_buf[island].astype(F32)
    for step in range(1, ni):
        await_count(step).wait_recv()
        tally = tally + c_buf[peer(step)].astype(F32)
    whole = tally[0:1, 0:1] * 256.0 + tally[8:9, 0:1]
    average = total / whole
    loads[6].wait()
    fresh = outer_beta * momentum[...] + average
    new_momentum[...] = fresh
    new_anchor[...] = anchor[...] - outer_rate * (average + outer_beta * fresh)

    for step in range(1, nf):
        send_hidden(step).wait_send()
    for step in range(1, ni):
        send_anchor(step).wait_send()
        send_count(step).wait_send()
        await_delta(step).wait_send()

    def drain(number, carry):
        turn = number // KVH
        head = number % KVH
        for step in range(1, nf):
            send_block(turn, head, step).wait_send()
            send_grad(turn, head, step).wait_send()
        return carry

    lax.fori_loop(0, 2 * KVH, drain, 0)


def on_device_any(*args):
    hidden, query, keys, _, _, first, _, anchor, _, _ = args
    ni = lax.axis_size("island")
    nf = lax.axis_size("fsdp")
    rows = hidden.shape[0]
    block, columns = anchor.shape
    if (rows, columns, ni, block) != (HD, HD // 2, 2 * KVH, 8 * HD):
        return on_device(*args)
    vmem = pl.BlockSpec(memory_space=pltpu.VMEM)
    anywhere = pl.BlockSpec(memory_space=pltpu.HBM)
    dma = pltpu.SemaphoreType.DMA
    args = args[:7] + (anchor.T, args[8].T, args[9])
    outs = pl.pallas_call(
        functools.partial(round_kernel, ni, nf),
        out_shape=[jax.ShapeDtypeStruct((columns, block), F32)] * 2,
        in_specs=[anywhere] * 4
        + [vmem]
        + [anywhere] * 4
        + [pl.BlockSpec(memory_space=pltpu.SMEM)],
        out_specs=[vmem, vmem],
        scratch_shapes=[
            pltpu.VMEM(query.shape, BF),
            pltpu.VMEM(query.shape, BF),
            pltpu.VMEM(keys.shape, BF),
            pltpu.VMEM((columns, block), F32),
            pltpu.VMEM((columns, block), F32),
            pltpu.VMEM(first.shape, F32),
            pltpu.VMEM(first.shape, F32),
            pltpu.VMEM((nf, rows, block), BF),
            pltpu.VMEM((block, nf * rows), BF),
            pltpu.VMEM((KVH, QPK * rows, rows), BF),
            pltpu.VMEM((KVH, rows, QPK * rows), BF),
            pltpu.VMEM((KVH, block, HD), BF),
            pltpu.VMEM((KVH, block, HD), F32),
            pltpu.VMEM((KVH, block, HD), F32),
            pltpu.VMEM((ni, columns, block), BF),
            pltpu.VMEM((ni, 16, 128), BF),
            pltpu.VMEM((2, KVH, nf, rows, HD), BF),
            pltpu.VMEM((2, KVH, nf, rows, HD), BF),
            pltpu.VMEM((2, KVH, nf * rows, HD), BF),
            pltpu.VMEM((ni, columns, block), BF),
            pltpu.VMEM((ni, columns, block), BF),
            dma((8,)),
            dma((nf,)),
            dma((nf,)),
            dma((ni,)),
            dma((ni,)),
            dma((ni,)),
            dma((ni,)),
            dma((2, KVH, nf)),
            dma((2, KVH, nf)),
            dma((2, KVH, nf)),
            dma((2, KVH, nf)),
            dma((ni,)),
            dma((ni,)),
        ],
        compiler_params=pltpu.CompilerParams(
            collective_id=0, has_side_effects=True, vmem_limit_bytes=62 * 2**20
        ),
    )(*args)
    return tuple(out.T for out in outs)


def solution(mesh):
    in_specs = (
        P(("island", "fsdp"), None),
        P(("island", "fsdp"), None),
        P(("island", "fsdp"), None),
        P(("island", "fsdp"), None),
        P(("island", "fsdp"), None),
        P("island", "fsdp", None),
        P("island", "fsdp", None),
        P("fsdp", "island"),
        P("fsdp", "island"),
        P("island"),
    )
    out_specs = (P("fsdp", "island"), P("fsdp", "island"))
    return jax.shard_map(
        on_device_any, mesh=mesh, in_specs=in_specs, out_specs=out_specs, check_vma=False
    )
```

```python
import functools
import math

import jax
import jax.numpy as jnp
from jax import lax
from jax.experimental import pallas as pl
from jax.experimental.pallas import tpu as pltpu
from jax.sharding import PartitionSpec as P

KVH = 4
QPK = 8
HD = 128


beta_one = 0.9
beta_two = 0.95
inner_rate = 0.05
decay = 0.1
epsilon = 1e-08
outer_rate = 0.7
outer_beta = 0.9


def attention_weights(query_rows, key_rows, segments):
    length = segments.shape[0]
    queries = query_rows.reshape(length, KVH, QPK, HD)
    keyed = key_rows.reshape(length, KVH, HD)
    scores = jnp.einsum("tgjd,sgd->gjts", queries, keyed, preferred_element_type=jnp.float32) * (
        1.0 / math.sqrt(HD)
    )
    place = jnp.arange(length)
    allowed = (place[None, :] <= place[:, None]) & (segments[:, None] == segments[None, :])
    scores = jnp.where(allowed[None, None], scores, -jnp.inf)
    highest = jnp.max(scores, axis=-1, keepdims=True)
    expo = jnp.exp(scores - highest)
    return (expo / jnp.sum(expo, axis=-1, keepdims=True)).astype(jnp.bfloat16)


def on_device(
    hidden,
    query_rows,
    key_rows,
    targets,
    segment_ids,
    first_moment,
    second_moment,
    anchor,
    outer_momentum,
    token_counts,
):
    rows = hidden.shape[0]
    width = key_rows.shape[1]
    group_rows = rows * lax.axis_size("fsdp")
    scale_in = 1.0 / math.sqrt(hidden.shape[1])
    attention = attention_weights(query_rows, key_rows, segment_ids[0])
    master = lax.all_gather(anchor, "island", axis=1, tiled=True)
    start_point = master
    block = master.shape[0]
    first = first_moment[0]
    second = second_moment[0]
    feature_rows = lax.all_to_all(hidden, "fsdp", split_axis=1, concat_axis=0, tiled=True)
    for inner_step in range(2):
        sent_rows = master.astype(jnp.bfloat16)
        blocks = jnp.dot(feature_rows, sent_rows, preferred_element_type=jnp.float32)
        pieces = lax.all_to_all(
            blocks.astype(jnp.bfloat16), "fsdp", split_axis=0, concat_axis=0, tiled=True
        )
        projected = jnp.sum(pieces.reshape(-1, rows, width).astype(jnp.float32), axis=0)
        values = (projected * scale_in).astype(jnp.bfloat16)
        mixed = jnp.einsum(
            "gjts,sgd->tgjd",
            attention,
            values.reshape(rows, KVH, HD),
            preferred_element_type=jnp.float32,
        )
        error = (
            (mixed.reshape(rows, KVH * QPK * HD) - targets.astype(jnp.float32)) / group_rows
        ).astype(jnp.bfloat16)
        back = jnp.einsum(
            "gjts,tgjd->sgd",
            attention,
            error.reshape(rows, KVH, QPK, HD),
            preferred_element_type=jnp.float32,
        )
        value_grad = (back.reshape(rows, width) * scale_in).astype(jnp.bfloat16)
        grad = lax.dot_general(
            feature_rows,
            lax.all_gather(value_grad, "fsdp", axis=0, tiled=True),
            (((0,), (0,)), ((), ())),
            preferred_element_type=jnp.float32,
        )
        first = beta_one * first + (1.0 - beta_one) * grad
        second = beta_two * second + (1.0 - beta_two) * grad * grad
        master = master - inner_rate * (first / (jnp.sqrt(second) + epsilon) + decay * master)
    delta = start_point - master
    groups = lax.axis_size("island")
    own_count = token_counts[0].astype(jnp.float32)
    total_count = lax.psum(own_count, "island")
    received = lax.all_to_all(
        own_count / total_count * delta, "island", split_axis=1, concat_axis=0, tiled=True
    )
    average = jnp.sum(received.reshape(groups, block, anchor.shape[1]), axis=0)
    new_momentum = outer_beta * outer_momentum + average
    new_anchor = anchor - outer_rate * (average + outer_beta * new_momentum)
    return (new_anchor, new_momentum)


MESH = pl.DeviceIdType.MESH
BF = jnp.bfloat16
F32 = jnp.float32


def dot(left, right):
    return jnp.dot(left, right, preferred_element_type=F32)


def round_kernel(
    ni,
    nf,
    hidden,
    query,
    keys_in,
    targets,
    segments,
    first_in,
    second_in,
    anchor_in,
    momentum_in,
    counts,
    new_anchor,
    new_momentum,
    q_buf,
    t_buf,
    keys,
    anchor,
    momentum,
    first,
    second,
    feat,
    feat_t,
    att,
    att_t,
    weight,
    master,
    delta,
    a_buf,
    c_buf,
    bv_send,
    bv_recv,
    vg_buf,
    d_send,
    d_recv,
    local_sem,
    h_send_sem,
    h_recv_sem,
    a_send_sem,
    a_recv_sem,
    c_send_sem,
    c_recv_sem,
    b_send_sem,
    b_recv_sem,
    v_send_sem,
    v_recv_sem,
    d_send_sem,
    d_recv_sem,
):
    me = lax.axis_index("fsdp")
    island = lax.axis_index("island")
    rows = feat.shape[1]
    block = feat.shape[2]
    columns = anchor.shape[0]
    group_rows = rows * nf
    scale_in = 1.0 / math.sqrt(hidden.shape[1])

    def ahead(step):
        return lax.rem(me + step, nf)

    def behind(step):
        return lax.rem(me + nf - step, nf)

    def peer(step):
        return lax.rem(island + step, ni)

    loads = [
        pltpu.make_async_copy(anchor_in, anchor, local_sem.at[0]),
        pltpu.make_async_copy(query, q_buf, local_sem.at[1]),
        pltpu.make_async_copy(targets, t_buf, local_sem.at[2]),
        pltpu.make_async_copy(first_in, first, local_sem.at[3]),
        pltpu.make_async_copy(second_in, second, local_sem.at[4]),
        pltpu.make_async_copy(keys_in, keys, local_sem.at[5]),
        pltpu.make_async_copy(momentum_in, momentum, local_sem.at[6]),
        pltpu.make_async_copy(
            hidden.at[:, pl.ds(pl.multiple_of(me * block, block), block)],
            feat.at[0],
            local_sem.at[7],
        ),
    ]
    for number in (0, 5, 1):
        loads[number].start()

    barrier = pltpu.get_barrier_semaphore()
    for step in range(1, nf):
        pl.semaphore_signal(
            barrier, inc=1, device_id=(island, ahead(step)), device_id_type=MESH
        )
    for step in range(1, ni):
        pl.semaphore_signal(barrier, inc=1, device_id=(peer(step), me), device_id_type=MESH)

    pl.semaphore_wait(barrier, ni + nf - 2)

    def send_hidden(step):
        return pltpu.make_async_remote_copy(
            src_ref=hidden.at[:, pl.ds(pl.multiple_of(ahead(step) * block, block), block)],
            dst_ref=feat.at[step],
            send_sem=h_send_sem.at[step],
            recv_sem=h_recv_sem.at[step],
            device_id=(island, ahead(step)),
            device_id_type=MESH,
        )

    def send_anchor(step):
        return pltpu.make_async_remote_copy(
            src_ref=a_buf.at[island],
            dst_ref=a_buf.at[island],
            send_sem=a_send_sem.at[step],
            recv_sem=a_recv_sem.at[island],
            device_id=(peer(step), me),
            device_id_type=MESH,
        )

    def await_anchor(step):
        owner = peer(step)
        return pltpu.make_async_remote_copy(
            src_ref=a_buf.at[owner],
            dst_ref=a_buf.at[owner],
            send_sem=a_send_sem.at[step],
            recv_sem=a_recv_sem.at[owner],
            device_id=(peer(step), me),
            device_id_type=MESH,
        )

    def send_count(step):
        return pltpu.make_async_remote_copy(
            src_ref=c_buf.at[island],
            dst_ref=c_buf.at[island],
            send_sem=c_send_sem.at[step],
            recv_sem=c_recv_sem.at[island],
            device_id=(peer(step), me),
            device_id_type=MESH,
        )

    def await_count(step):
        owner = peer(step)
        return pltpu.make_async_remote_copy(
            src_ref=c_buf.at[owner],
            dst_ref=c_buf.at[owner],
            send_sem=c_send_sem.at[step],
            recv_sem=c_recv_sem.at[owner],
            device_id=(owner, me),
            device_id_type=MESH,
        )

    def order(number):
        return lax.rem(number + island // 2, KVH)

    def send_block(turn, head, step):
        return pltpu.make_async_remote_copy(
            src_ref=bv_send.at[turn, head, step],
            dst_ref=bv_recv.at[turn, head, step],
            send_sem=b_send_sem.at[turn, head, step],
            recv_sem=b_recv_sem.at[turn, head, step],
            device_id=(island, behind(step)),
            device_id_type=MESH,
        )

    def send_grad(turn, head, step):
        return pltpu.make_async_remote_copy(
            src_ref=vg_buf.at[turn, head, 0:rows],
            dst_ref=vg_buf.at[turn, head, step * rows : (step + 1) * rows],
            send_sem=v_send_sem.at[turn, head, step],
            recv_sem=v_recv_sem.at[turn, head, step],
            device_id=(island, ahead(step)),
            device_id_type=MESH,
        )

    def send_delta(owner):
        return pltpu.make_async_remote_copy(
            src_ref=d_send.at[owner],
            dst_ref=d_recv.at[island],
            send_sem=d_send_sem.at[owner],
            recv_sem=d_recv_sem.at[island],
            device_id=(owner, me),
            device_id_type=MESH,
        )

    def await_delta(step):
        owner = peer(step)
        return pltpu.make_async_remote_copy(
            src_ref=d_send.at[owner],
            dst_ref=d_recv.at[owner],
            send_sem=d_send_sem.at[owner],
            recv_sem=d_recv_sem.at[owner],
            device_id=(owner, me),
            device_id_type=MESH,
        )

    near_first = [1, 3, 2] if nf == 4 else list(range(1, nf))
    for step in near_first:
        send_hidden(step).start()
    loads[0].wait()
    a_buf[island] = anchor[...].astype(BF)
    count = counts[0]
    high = (count // 256).astype(F32)
    low = (count % 256).astype(F32)
    upper = lax.broadcasted_iota(jnp.int32, (16, 128), 0) < 8
    c_buf[island] = jnp.where(upper, high, low).astype(BF)
    for step in range(1, ni):
        send_anchor(step).start()
        send_count(step).start()
    for number in (7, 2, 3, 4, 6):
        loads[number].start()

    loads[5].wait()
    loads[1].wait()
    seg = jnp.broadcast_to(segments[...].astype(F32), (rows, rows))
    place_t = lax.broadcasted_iota(jnp.int32, (rows, rows), 0)
    place_s = lax.broadcasted_iota(jnp.int32, (rows, rows), 1)
    allowed = (place_s <= place_t) & (seg == seg.T)

    def attend(number, carry):
        head = number // QPK
        within = number % QPK
        queries = q_buf[:, pl.ds(pl.multiple_of(number * HD, HD), HD)]
        keyed = keys[:, pl.ds(pl.multiple_of(head * HD, HD), HD)]
        scores = lax.dot_general(
            queries, keyed, (((1,), (1,)), ((), ())), preferred_element_type=F32
        ) * (1.0 / math.sqrt(HD))
        scores = jnp.where(allowed, scores, -1e30)
        expo = jnp.exp(scores - jnp.max(scores, axis=1, keepdims=True))
        ratio = expo / jnp.sum(expo, axis=1, keepdims=True)
        at = pl.ds(pl.multiple_of(within * rows, rows), rows)
        att[head, at, :] = ratio.astype(BF)
        att_t[head, :, at] = ratio.T.astype(BF)
        return carry

    lax.fori_loop(0, KVH * QPK, attend, 0, unroll=2)

    for step in range(1, ni):
        await_anchor(step).wait_recv()

    def merge(head, carry):
        both = jnp.concatenate([a_buf[2 * head], a_buf[2 * head + 1]], axis=0).T
        weight[head] = both
        master[head] = both.astype(F32)
        return carry

    lax.fori_loop(0, KVH, merge, 0)

    for step in [0] + near_first:
        if step == 0:
            loads[7].wait()
        else:
            send_hidden(step).wait_recv()

        def first_blocks(number, carry, step=step):
            head = order(number)
            piece = dot(feat[step], weight[head]).astype(BF)
            if step == 0:
                bv_recv[0, head, 0] = piece
            else:
                bv_send[0, head, step] = piece
                send_block(0, head, step).start()
            return carry

        lax.fori_loop(0, KVH, first_blocks, 0)
    for step in range(nf):
        feat_t[:, step * rows : (step + 1) * rows] = feat[step].T

    def attention_turn(turn, head):
        for step in range(1, nf):
            send_block(turn, head, step).wait_recv()
        projected = bv_recv[turn, head, 0].astype(F32)
        for step in range(1, nf):
            projected = projected + bv_recv[turn, head, step].astype(F32)
        values = (projected * scale_in).astype(BF)
        back = jnp.zeros((rows, HD), F32)
        for within in range(QPK):
            lot = slice(within * rows, (within + 1) * rows)
            mixed = dot(att[head, lot, :], values)
            aim = t_buf[:, pl.ds(pl.multiple_of((head * QPK + within) * HD, HD), HD)]
            error = ((mixed - aim.astype(F32)) * (1.0 / group_rows)).astype(BF)
            back = back + dot(att_t[head, :, lot], error)
        vg_buf[turn, head, 0:rows] = (back * scale_in).astype(BF)
        for step in near_first:
            send_grad(turn, head, step).start()

    def update_turn(turn, head):
        for step in range(1, nf):
            send_grad(turn, head, step).wait_recv()
        lanes = pl.ds(pl.multiple_of(head * HD, HD), HD)
        part = block // 4

        def rows_part(index, carry):
            at = pl.ds(pl.multiple_of(index * part, part), part)
            grad = dot(feat_t[at, :], vg_buf[turn, head])
            one = beta_one * first[0, at, lanes] + (1.0 - beta_one) * grad
            two = beta_two * second[0, at, lanes] + (1.0 - beta_two) * grad * grad
            now = master[head, at]
            move = inner_rate * (one / (jnp.sqrt(two) + epsilon) + decay * now)
            if turn == 0:
                first[0, at, lanes] = one
                second[0, at, lanes] = two
                delta[head, at] = move
                later = now - move
                master[head, at] = later
                weight[head, at] = later.astype(BF)
            else:
                delta[head, at] = (delta[head, at] + move) * count.astype(F32)
            return carry

        lax.fori_loop(0, 4, rows_part, 0)

    def turn_one_attention(number, carry):
        head = order(number)
        attention_turn(0, head)
        return carry

    def turn_one_update(number, carry):
        head = order(number)
        update_turn(0, head)
        whole_blocks = dot(feat[...].reshape(nf * rows, block), weight[head]).astype(BF)
        for step in [2, 1, 3, 0] if nf == 4 else list(range(nf)):
            piece = whole_blocks[step * rows : (step + 1) * rows]
            if step == 0:
                bv_recv[1, head, 0] = piece
            else:
                bv_send[1, head, step] = piece
                send_block(1, head, step).start()
        return carry

    def turn_two_attention(number, carry):
        head = order(number)
        attention_turn(1, head)
        return carry

    def turn_two_update(number, carry):
        head = order(number)
        update_turn(1, head)
        turned = delta[head].astype(BF).T
        d_send[2 * head] = turned[:columns]
        d_send[2 * head + 1] = turned[columns:]
        for odd in range(2):
            owner = 2 * head + odd

            @pl.when(owner != island)
            def _():
                send_delta(owner).start()

        return carry

    loads[2].wait()
    lax.fori_loop(0, KVH, turn_one_attention, 0)
    loads[3].wait()
    loads[4].wait()
    lax.fori_loop(0, KVH, turn_one_update, 0)
    lax.fori_loop(0, KVH, turn_two_attention, 0)
    lax.fori_loop(0, KVH, turn_two_update, 0)

    for step in range(1, ni):
        await_delta(step).wait_recv()
    total = d_send[island].astype(F32)
    for step in range(1, ni):
        total = total + d_recv[peer(step)].astype(F32)
    tally = c_buf[island].astype(F32)
    for step in range(1, ni):
        await_count(step).wait_recv()
        tally = tally + c_buf[peer(step)].astype(F32)
    whole = tally[0:1, 0:1] * 256.0 + tally[8:9, 0:1]
    average = total / whole
    loads[6].wait()
    fresh = outer_beta * momentum[...] + average
    new_momentum[...] = fresh
    new_anchor[...] = anchor[...] - outer_rate * (average + outer_beta * fresh)

    for step in range(1, nf):
        send_hidden(step).wait_send()
    for step in range(1, ni):
        send_anchor(step).wait_send()
        send_count(step).wait_send()
        await_delta(step).wait_send()

    def drain(number, carry):
        turn = number // KVH
        head = number % KVH
        for step in range(1, nf):
            send_block(turn, head, step).wait_send()
            send_grad(turn, head, step).wait_send()
        return carry

    lax.fori_loop(0, 2 * KVH, drain, 0)


def on_device_any(*args):
    hidden, query, keys, _, _, first, _, anchor, _, _ = args
    ni = lax.axis_size("island")
    nf = lax.axis_size("fsdp")
    rows = hidden.shape[0]
    block, columns = anchor.shape
    if (rows, columns, ni, block) != (HD, HD // 2, 2 * KVH, 8 * HD):
        return on_device(*args)
    vmem = pl.BlockSpec(memory_space=pltpu.VMEM)
    anywhere = pl.BlockSpec(memory_space=pltpu.HBM)
    dma = pltpu.SemaphoreType.DMA
    args = args[:7] + (anchor.T, args[8].T, args[9])
    outs = pl.pallas_call(
        functools.partial(round_kernel, ni, nf),
        out_shape=[jax.ShapeDtypeStruct((columns, block), F32)] * 2,
        in_specs=[anywhere] * 4
        + [vmem]
        + [anywhere] * 4
        + [pl.BlockSpec(memory_space=pltpu.SMEM)],
        out_specs=[vmem, vmem],
        scratch_shapes=[
            pltpu.VMEM(query.shape, BF),
            pltpu.VMEM(query.shape, BF),
            pltpu.VMEM(keys.shape, BF),
            pltpu.VMEM((columns, block), F32),
            pltpu.VMEM((columns, block), F32),
            pltpu.VMEM(first.shape, F32),
            pltpu.VMEM(first.shape, F32),
            pltpu.VMEM((nf, rows, block), BF),
            pltpu.VMEM((block, nf * rows), BF),
            pltpu.VMEM((KVH, QPK * rows, rows), BF),
            pltpu.VMEM((KVH, rows, QPK * rows), BF),
            pltpu.VMEM((KVH, block, HD), BF),
            pltpu.VMEM((KVH, block, HD), F32),
            pltpu.VMEM((KVH, block, HD), F32),
            pltpu.VMEM((ni, columns, block), BF),
            pltpu.VMEM((ni, 16, 128), BF),
            pltpu.VMEM((2, KVH, nf, rows, HD), BF),
            pltpu.VMEM((2, KVH, nf, rows, HD), BF),
            pltpu.VMEM((2, KVH, nf * rows, HD), BF),
            pltpu.VMEM((ni, columns, block), BF),
            pltpu.VMEM((ni, columns, block), BF),
            dma((8,)),
            dma((nf,)),
            dma((nf,)),
            dma((ni,)),
            dma((ni,)),
            dma((ni,)),
            dma((ni,)),
            dma((2, KVH, nf)),
            dma((2, KVH, nf)),
            dma((2, KVH, nf)),
            dma((2, KVH, nf)),
            dma((ni,)),
            dma((ni,)),
        ],
        compiler_params=pltpu.CompilerParams(
            collective_id=0, has_side_effects=True, vmem_limit_bytes=62 * 2**20
        ),
    )(*args)
    return tuple(out.T for out in outs)


def solution(mesh):
    in_specs = (
        P(("island", "fsdp"), None),
        P(("island", "fsdp"), None),
        P(("island", "fsdp"), None),
        P(("island", "fsdp"), None),
        P(("island", "fsdp"), None),
        P("island", "fsdp", None),
        P("island", "fsdp", None),
        P("fsdp", "island"),
        P("fsdp", "island"),
        P("island"),
    )
    out_specs = (P("fsdp", "island"), P("fsdp", "island"))
    return jax.shard_map(
        on_device_any, mesh=mesh, in_specs=in_specs, out_specs=out_specs, check_vma=False
    )
```

```python
import functools
import math

import jax
import jax.numpy as jnp
from jax import lax
from jax.experimental import pallas as pl
from jax.experimental.pallas import tpu as pltpu
from jax.sharding import PartitionSpec as P

KVH = 4
QPK = 8
HD = 128


beta_one = 0.9
beta_two = 0.95
inner_rate = 0.05
decay = 0.1
epsilon = 1e-08
outer_rate = 0.7
outer_beta = 0.9


def attention_weights(query_rows, key_rows, segments):
    length = segments.shape[0]
    queries = query_rows.reshape(length, KVH, QPK, HD)
    keyed = key_rows.reshape(length, KVH, HD)
    scores = jnp.einsum("tgjd,sgd->gjts", queries, keyed, preferred_element_type=jnp.float32) * (
        1.0 / math.sqrt(HD)
    )
    place = jnp.arange(length)
    allowed = (place[None, :] <= place[:, None]) & (segments[:, None] == segments[None, :])
    scores = jnp.where(allowed[None, None], scores, -jnp.inf)
    highest = jnp.max(scores, axis=-1, keepdims=True)
    expo = jnp.exp(scores - highest)
    return (expo / jnp.sum(expo, axis=-1, keepdims=True)).astype(jnp.bfloat16)


def on_device(
    hidden,
    query_rows,
    key_rows,
    targets,
    segment_ids,
    first_moment,
    second_moment,
    anchor,
    outer_momentum,
    token_counts,
):
    rows = hidden.shape[0]
    width = key_rows.shape[1]
    group_rows = rows * lax.axis_size("fsdp")
    scale_in = 1.0 / math.sqrt(hidden.shape[1])
    attention = attention_weights(query_rows, key_rows, segment_ids[0])
    master = lax.all_gather(anchor, "island", axis=1, tiled=True)
    start_point = master
    block = master.shape[0]
    first = first_moment[0]
    second = second_moment[0]
    feature_rows = lax.all_to_all(hidden, "fsdp", split_axis=1, concat_axis=0, tiled=True)
    for inner_step in range(2):
        sent_rows = master.astype(jnp.bfloat16)
        blocks = jnp.dot(feature_rows, sent_rows, preferred_element_type=jnp.float32)
        pieces = lax.all_to_all(
            blocks.astype(jnp.bfloat16), "fsdp", split_axis=0, concat_axis=0, tiled=True
        )
        projected = jnp.sum(pieces.reshape(-1, rows, width).astype(jnp.float32), axis=0)
        values = (projected * scale_in).astype(jnp.bfloat16)
        mixed = jnp.einsum(
            "gjts,sgd->tgjd",
            attention,
            values.reshape(rows, KVH, HD),
            preferred_element_type=jnp.float32,
        )
        error = (
            (mixed.reshape(rows, KVH * QPK * HD) - targets.astype(jnp.float32)) / group_rows
        ).astype(jnp.bfloat16)
        back = jnp.einsum(
            "gjts,tgjd->sgd",
            attention,
            error.reshape(rows, KVH, QPK, HD),
            preferred_element_type=jnp.float32,
        )
        value_grad = (back.reshape(rows, width) * scale_in).astype(jnp.bfloat16)
        grad = lax.dot_general(
            feature_rows,
            lax.all_gather(value_grad, "fsdp", axis=0, tiled=True),
            (((0,), (0,)), ((), ())),
            preferred_element_type=jnp.float32,
        )
        first = beta_one * first + (1.0 - beta_one) * grad
        second = beta_two * second + (1.0 - beta_two) * grad * grad
        master = master - inner_rate * (first / (jnp.sqrt(second) + epsilon) + decay * master)
    delta = start_point - master
    groups = lax.axis_size("island")
    own_count = token_counts[0].astype(jnp.float32)
    total_count = lax.psum(own_count, "island")
    received = lax.all_to_all(
        own_count / total_count * delta, "island", split_axis=1, concat_axis=0, tiled=True
    )
    average = jnp.sum(received.reshape(groups, block, anchor.shape[1]), axis=0)
    new_momentum = outer_beta * outer_momentum + average
    new_anchor = anchor - outer_rate * (average + outer_beta * new_momentum)
    return (new_anchor, new_momentum)


MESH = pl.DeviceIdType.MESH
BF = jnp.bfloat16
F32 = jnp.float32


def dot(left, right):
    return jnp.dot(left, right, preferred_element_type=F32)


def round_kernel(
    ni,
    nf,
    hidden,
    query,
    keys_in,
    targets,
    segments,
    first_in,
    second_in,
    anchor_in,
    momentum_in,
    counts,
    new_anchor,
    new_momentum,
    q_buf,
    t_buf,
    keys,
    anchor,
    momentum,
    first,
    second,
    feat,
    feat_t,
    att,
    att_t,
    weight,
    master,
    delta,
    a_buf,
    c_buf,
    bv_send,
    bv_recv,
    vg_buf,
    d_send,
    d_recv,
    local_sem,
    h_send_sem,
    h_recv_sem,
    a_send_sem,
    a_recv_sem,
    c_send_sem,
    c_recv_sem,
    b_send_sem,
    b_recv_sem,
    v_send_sem,
    v_recv_sem,
    d_send_sem,
    d_recv_sem,
):
    me = lax.axis_index("fsdp")
    island = lax.axis_index("island")
    rows = feat.shape[1]
    block = feat.shape[2]
    columns = anchor.shape[0]
    group_rows = rows * nf
    scale_in = 1.0 / math.sqrt(hidden.shape[1])

    def ahead(step):
        return lax.rem(me + step, nf)

    def behind(step):
        return lax.rem(me + nf - step, nf)

    def peer(step):
        return lax.rem(island + step, ni)

    loads = [
        pltpu.make_async_copy(anchor_in, anchor, local_sem.at[0]),
        pltpu.make_async_copy(query, q_buf, local_sem.at[1]),
        pltpu.make_async_copy(targets, t_buf, local_sem.at[2]),
        pltpu.make_async_copy(first_in, first, local_sem.at[3]),
        pltpu.make_async_copy(second_in, second, local_sem.at[4]),
        pltpu.make_async_copy(keys_in, keys, local_sem.at[5]),
        pltpu.make_async_copy(momentum_in, momentum, local_sem.at[6]),
        pltpu.make_async_copy(
            hidden.at[:, pl.ds(pl.multiple_of(me * block, block), block)],
            feat.at[0],
            local_sem.at[7],
        ),
    ]
    for number in (0, 5, 1):
        loads[number].start()

    barrier = pltpu.get_barrier_semaphore()
    for step in range(1, nf):
        pl.semaphore_signal(
            barrier, inc=1, device_id=(island, ahead(step)), device_id_type=MESH
        )
    for step in range(1, ni):
        pl.semaphore_signal(barrier, inc=1, device_id=(peer(step), me), device_id_type=MESH)

    pl.semaphore_wait(barrier, ni + nf - 2)

    def send_hidden(step):
        return pltpu.make_async_remote_copy(
            src_ref=hidden.at[:, pl.ds(pl.multiple_of(ahead(step) * block, block), block)],
            dst_ref=feat.at[step],
            send_sem=h_send_sem.at[step],
            recv_sem=h_recv_sem.at[step],
            device_id=(island, ahead(step)),
            device_id_type=MESH,
        )

    def send_anchor(step):
        return pltpu.make_async_remote_copy(
            src_ref=a_buf.at[island],
            dst_ref=a_buf.at[island],
            send_sem=a_send_sem.at[step],
            recv_sem=a_recv_sem.at[island],
            device_id=(peer(step), me),
            device_id_type=MESH,
        )

    def await_anchor(step):
        owner = peer(step)
        return pltpu.make_async_remote_copy(
            src_ref=a_buf.at[owner],
            dst_ref=a_buf.at[owner],
            send_sem=a_send_sem.at[step],
            recv_sem=a_recv_sem.at[owner],
            device_id=(peer(step), me),
            device_id_type=MESH,
        )

    def send_count(step):
        return pltpu.make_async_remote_copy(
            src_ref=c_buf.at[island],
            dst_ref=c_buf.at[island],
            send_sem=c_send_sem.at[step],
            recv_sem=c_recv_sem.at[island],
            device_id=(peer(step), me),
            device_id_type=MESH,
        )

    def await_count(step):
        owner = peer(step)
        return pltpu.make_async_remote_copy(
            src_ref=c_buf.at[owner],
            dst_ref=c_buf.at[owner],
            send_sem=c_send_sem.at[step],
            recv_sem=c_recv_sem.at[owner],
            device_id=(owner, me),
            device_id_type=MESH,
        )

    def order(number):
        return lax.rem(number + island // 2, KVH)

    def send_block(turn, head, step):
        return pltpu.make_async_remote_copy(
            src_ref=bv_send.at[turn, head, step],
            dst_ref=bv_recv.at[turn, head, step],
            send_sem=b_send_sem.at[turn, head, step],
            recv_sem=b_recv_sem.at[turn, head, step],
            device_id=(island, behind(step)),
            device_id_type=MESH,
        )

    def send_grad(turn, head, step):
        return pltpu.make_async_remote_copy(
            src_ref=vg_buf.at[turn, head, 0:rows],
            dst_ref=vg_buf.at[turn, head, step * rows : (step + 1) * rows],
            send_sem=v_send_sem.at[turn, head, step],
            recv_sem=v_recv_sem.at[turn, head, step],
            device_id=(island, ahead(step)),
            device_id_type=MESH,
        )

    def send_delta(owner):
        return pltpu.make_async_remote_copy(
            src_ref=d_send.at[owner],
            dst_ref=d_recv.at[island],
            send_sem=d_send_sem.at[owner],
            recv_sem=d_recv_sem.at[island],
            device_id=(owner, me),
            device_id_type=MESH,
        )

    def await_delta(step):
        owner = peer(step)
        return pltpu.make_async_remote_copy(
            src_ref=d_send.at[owner],
            dst_ref=d_recv.at[owner],
            send_sem=d_send_sem.at[owner],
            recv_sem=d_recv_sem.at[owner],
            device_id=(owner, me),
            device_id_type=MESH,
        )

    near_first = [1, 3, 2] if nf == 4 else list(range(1, nf))
    for step in near_first:
        send_hidden(step).start()
    loads[0].wait()
    a_buf[island] = anchor[...].astype(BF)
    count = counts[0]
    high = (count // 256).astype(F32)
    low = (count % 256).astype(F32)
    upper = lax.broadcasted_iota(jnp.int32, (16, 128), 0) < 8
    c_buf[island] = jnp.where(upper, high, low).astype(BF)
    for step in range(1, ni):
        send_anchor(step).start()
        send_count(step).start()
    for number in (7, 2, 3, 4, 6):
        loads[number].start()

    loads[5].wait()
    loads[1].wait()
    seg = jnp.broadcast_to(segments[...].astype(F32), (rows, rows))
    place_t = lax.broadcasted_iota(jnp.int32, (rows, rows), 0)
    place_s = lax.broadcasted_iota(jnp.int32, (rows, rows), 1)
    allowed = (place_s <= place_t) & (seg == seg.T)

    def attend(number, carry):
        head = number // QPK
        within = number % QPK
        queries = q_buf[:, pl.ds(pl.multiple_of(number * HD, HD), HD)]
        keyed = keys[:, pl.ds(pl.multiple_of(head * HD, HD), HD)]
        scores = lax.dot_general(
            queries, keyed, (((1,), (1,)), ((), ())), preferred_element_type=F32
        ) * (1.0 / math.sqrt(HD))
        scores = jnp.where(allowed, scores, -1e30)
        expo = jnp.exp(scores - jnp.max(scores, axis=1, keepdims=True))
        ratio = expo / jnp.sum(expo, axis=1, keepdims=True)
        at = pl.ds(pl.multiple_of(within * rows, rows), rows)
        att[head, at, :] = ratio.astype(BF)
        att_t[head, :, at] = ratio.T.astype(BF)
        return carry

    lax.fori_loop(0, KVH * QPK, attend, 0, unroll=2)

    for step in range(1, ni):
        await_anchor(step).wait_recv()

    def merge(head, carry):
        both = jnp.concatenate([a_buf[2 * head], a_buf[2 * head + 1]], axis=0).T
        weight[head] = both
        master[head] = both.astype(F32)
        return carry

    lax.fori_loop(0, KVH, merge, 0)

    for step in [0] + near_first:
        if step == 0:
            loads[7].wait()
        else:
            send_hidden(step).wait_recv()

        def first_blocks(number, carry, step=step):
            head = order(number)
            piece = dot(feat[step], weight[head]).astype(BF)
            if step == 0:
                bv_recv[0, head, 0] = piece
            else:
                bv_send[0, head, step] = piece
                send_block(0, head, step).start()
            return carry

        lax.fori_loop(0, KVH, first_blocks, 0)
    for step in range(nf):
        feat_t[:, step * rows : (step + 1) * rows] = feat[step].T

    def attention_turn(turn, head):
        for step in range(1, nf):
            send_block(turn, head, step).wait_recv()
        projected = bv_recv[turn, head, 0].astype(F32)
        for step in range(1, nf):
            projected = projected + bv_recv[turn, head, step].astype(F32)
        values = (projected * scale_in).astype(BF)
        back = jnp.zeros((rows, HD), F32)
        for within in range(QPK):
            lot = slice(within * rows, (within + 1) * rows)
            mixed = dot(att[head, lot, :], values)
            aim = t_buf[:, pl.ds(pl.multiple_of((head * QPK + within) * HD, HD), HD)]
            error = ((mixed - aim.astype(F32)) * (1.0 / group_rows)).astype(BF)
            back = back + dot(att_t[head, :, lot], error)
        vg_buf[turn, head, 0:rows] = (back * scale_in).astype(BF)
        for step in near_first:
            send_grad(turn, head, step).start()

    def update_turn(turn, head):
        for step in range(1, nf):
            send_grad(turn, head, step).wait_recv()
        lanes = pl.ds(pl.multiple_of(head * HD, HD), HD)
        part = block // 4

        def rows_part(index, carry):
            at = pl.ds(pl.multiple_of(index * part, part), part)
            grad = dot(feat_t[at, :], vg_buf[turn, head])
            one = beta_one * first[0, at, lanes] + (1.0 - beta_one) * grad
            two = beta_two * second[0, at, lanes] + (1.0 - beta_two) * grad * grad
            now = master[head, at]
            move = inner_rate * (one / (jnp.sqrt(two) + epsilon) + decay * now)
            if turn == 0:
                first[0, at, lanes] = one
                second[0, at, lanes] = two
                delta[head, at] = move
                later = now - move
                master[head, at] = later
                weight[head, at] = later.astype(BF)
            else:
                delta[head, at] = (delta[head, at] + move) * count.astype(F32)
            return carry

        lax.fori_loop(0, 4, rows_part, 0)

    def turn_one_attention(number, carry):
        head = order(number)
        attention_turn(0, head)
        return carry

    def turn_one_update(number, carry):
        head = order(number)
        update_turn(0, head)
        for step in [1, 3, 2, 0] if nf == 4 else list(range(nf)):
            piece = dot(feat[step], weight[head]).astype(BF)
            if step == 0:
                bv_recv[1, head, 0] = piece
            else:
                bv_send[1, head, step] = piece
                send_block(1, head, step).start()
        return carry

    def turn_two_attention(number, carry):
        head = order(number)
        attention_turn(1, head)
        return carry

    def turn_two_update(number, carry):
        head = order(number)
        update_turn(1, head)
        turned = delta[head].astype(BF).T
        d_send[2 * head] = turned[:columns]
        d_send[2 * head + 1] = turned[columns:]
        for odd in range(2):
            owner = 2 * head + odd

            @pl.when(owner != island)
            def _():
                send_delta(owner).start()

        return carry

    loads[2].wait()
    lax.fori_loop(0, KVH, turn_one_attention, 0)
    loads[3].wait()
    loads[4].wait()
    turn_one_update(0, 0)

    def crossed(number, carry):
        turn_one_update(number, carry)
        turn_two_attention(number - 1, carry)
        return carry

    lax.fori_loop(1, KVH, crossed, 0)
    turn_two_update(0, 0)
    turn_two_attention(KVH - 1, 0)
    lax.fori_loop(1, KVH, turn_two_update, 0)

    for step in range(1, ni):
        await_delta(step).wait_recv()
    total = d_send[island].astype(F32)
    for step in range(1, ni):
        total = total + d_recv[peer(step)].astype(F32)
    tally = c_buf[island].astype(F32)
    for step in range(1, ni):
        await_count(step).wait_recv()
        tally = tally + c_buf[peer(step)].astype(F32)
    whole = tally[0:1, 0:1] * 256.0 + tally[8:9, 0:1]
    average = total / whole
    loads[6].wait()
    fresh = outer_beta * momentum[...] + average
    new_momentum[...] = fresh
    new_anchor[...] = anchor[...] - outer_rate * (average + outer_beta * fresh)

    for step in range(1, nf):
        send_hidden(step).wait_send()
    for step in range(1, ni):
        send_anchor(step).wait_send()
        send_count(step).wait_send()
        await_delta(step).wait_send()

    def drain(number, carry):
        turn = number // KVH
        head = number % KVH
        for step in range(1, nf):
            send_block(turn, head, step).wait_send()
            send_grad(turn, head, step).wait_send()
        return carry

    lax.fori_loop(0, 2 * KVH, drain, 0)


def on_device_any(*args):
    hidden, query, keys, _, _, first, _, anchor, _, _ = args
    ni = lax.axis_size("island")
    nf = lax.axis_size("fsdp")
    rows = hidden.shape[0]
    block, columns = anchor.shape
    if (rows, columns, ni, block) != (HD, HD // 2, 2 * KVH, 8 * HD):
        return on_device(*args)
    vmem = pl.BlockSpec(memory_space=pltpu.VMEM)
    anywhere = pl.BlockSpec(memory_space=pltpu.HBM)
    dma = pltpu.SemaphoreType.DMA
    args = args[:7] + (anchor.T, args[8].T, args[9])
    outs = pl.pallas_call(
        functools.partial(round_kernel, ni, nf),
        out_shape=[jax.ShapeDtypeStruct((columns, block), F32)] * 2,
        in_specs=[anywhere] * 4
        + [vmem]
        + [anywhere] * 4
        + [pl.BlockSpec(memory_space=pltpu.SMEM)],
        out_specs=[vmem, vmem],
        scratch_shapes=[
            pltpu.VMEM(query.shape, BF),
            pltpu.VMEM(query.shape, BF),
            pltpu.VMEM(keys.shape, BF),
            pltpu.VMEM((columns, block), F32),
            pltpu.VMEM((columns, block), F32),
            pltpu.VMEM(first.shape, F32),
            pltpu.VMEM(first.shape, F32),
            pltpu.VMEM((nf, rows, block), BF),
            pltpu.VMEM((block, nf * rows), BF),
            pltpu.VMEM((KVH, QPK * rows, rows), BF),
            pltpu.VMEM((KVH, rows, QPK * rows), BF),
            pltpu.VMEM((KVH, block, HD), BF),
            pltpu.VMEM((KVH, block, HD), F32),
            pltpu.VMEM((KVH, block, HD), F32),
            pltpu.VMEM((ni, columns, block), BF),
            pltpu.VMEM((ni, 16, 128), BF),
            pltpu.VMEM((2, KVH, nf, rows, HD), BF),
            pltpu.VMEM((2, KVH, nf, rows, HD), BF),
            pltpu.VMEM((2, KVH, nf * rows, HD), BF),
            pltpu.VMEM((ni, columns, block), BF),
            pltpu.VMEM((ni, columns, block), BF),
            dma((8,)),
            dma((nf,)),
            dma((nf,)),
            dma((ni,)),
            dma((ni,)),
            dma((ni,)),
            dma((ni,)),
            dma((2, KVH, nf)),
            dma((2, KVH, nf)),
            dma((2, KVH, nf)),
            dma((2, KVH, nf)),
            dma((ni,)),
            dma((ni,)),
        ],
        compiler_params=pltpu.CompilerParams(
            collective_id=0, has_side_effects=True, vmem_limit_bytes=62 * 2**20
        ),
    )(*args)
    return tuple(out.T for out in outs)


def solution(mesh):
    in_specs = (
        P(("island", "fsdp"), None),
        P(("island", "fsdp"), None),
        P(("island", "fsdp"), None),
        P(("island", "fsdp"), None),
        P(("island", "fsdp"), None),
        P("island", "fsdp", None),
        P("island", "fsdp", None),
        P("fsdp", "island"),
        P("fsdp", "island"),
        P("island"),
    )
    out_specs = (P("fsdp", "island"), P("fsdp", "island"))
    return jax.shard_map(
        on_device_any, mesh=mesh, in_specs=in_specs, out_specs=out_specs, check_vma=False
    )
```

```python
import functools
import math

import jax
import jax.numpy as jnp
from jax import lax
from jax.experimental import pallas as pl
from jax.experimental.pallas import tpu as pltpu
from jax.sharding import PartitionSpec as P

KVH = 4
QPK = 8
HD = 128


beta_one = 0.9
beta_two = 0.95
inner_rate = 0.05
decay = 0.1
epsilon = 1e-08
outer_rate = 0.7
outer_beta = 0.9


def attention_weights(query_rows, key_rows, segments):
    length = segments.shape[0]
    queries = query_rows.reshape(length, KVH, QPK, HD)
    keyed = key_rows.reshape(length, KVH, HD)
    scores = jnp.einsum("tgjd,sgd->gjts", queries, keyed, preferred_element_type=jnp.float32) * (
        1.0 / math.sqrt(HD)
    )
    place = jnp.arange(length)
    allowed = (place[None, :] <= place[:, None]) & (segments[:, None] == segments[None, :])
    scores = jnp.where(allowed[None, None], scores, -jnp.inf)
    highest = jnp.max(scores, axis=-1, keepdims=True)
    expo = jnp.exp(scores - highest)
    return (expo / jnp.sum(expo, axis=-1, keepdims=True)).astype(jnp.bfloat16)


def on_device(
    hidden,
    query_rows,
    key_rows,
    targets,
    segment_ids,
    first_moment,
    second_moment,
    anchor,
    outer_momentum,
    token_counts,
):
    rows = hidden.shape[0]
    width = key_rows.shape[1]
    group_rows = rows * lax.axis_size("fsdp")
    scale_in = 1.0 / math.sqrt(hidden.shape[1])
    attention = attention_weights(query_rows, key_rows, segment_ids[0])
    master = lax.all_gather(anchor, "island", axis=1, tiled=True)
    start_point = master
    block = master.shape[0]
    first = first_moment[0]
    second = second_moment[0]
    feature_rows = lax.all_to_all(hidden, "fsdp", split_axis=1, concat_axis=0, tiled=True)
    for inner_step in range(2):
        sent_rows = master.astype(jnp.bfloat16)
        blocks = jnp.dot(feature_rows, sent_rows, preferred_element_type=jnp.float32)
        pieces = lax.all_to_all(
            blocks.astype(jnp.bfloat16), "fsdp", split_axis=0, concat_axis=0, tiled=True
        )
        projected = jnp.sum(pieces.reshape(-1, rows, width).astype(jnp.float32), axis=0)
        values = (projected * scale_in).astype(jnp.bfloat16)
        mixed = jnp.einsum(
            "gjts,sgd->tgjd",
            attention,
            values.reshape(rows, KVH, HD),
            preferred_element_type=jnp.float32,
        )
        error = (
            (mixed.reshape(rows, KVH * QPK * HD) - targets.astype(jnp.float32)) / group_rows
        ).astype(jnp.bfloat16)
        back = jnp.einsum(
            "gjts,tgjd->sgd",
            attention,
            error.reshape(rows, KVH, QPK, HD),
            preferred_element_type=jnp.float32,
        )
        value_grad = (back.reshape(rows, width) * scale_in).astype(jnp.bfloat16)
        grad = lax.dot_general(
            feature_rows,
            lax.all_gather(value_grad, "fsdp", axis=0, tiled=True),
            (((0,), (0,)), ((), ())),
            preferred_element_type=jnp.float32,
        )
        first = beta_one * first + (1.0 - beta_one) * grad
        second = beta_two * second + (1.0 - beta_two) * grad * grad
        master = master - inner_rate * (first / (jnp.sqrt(second) + epsilon) + decay * master)
    delta = start_point - master
    groups = lax.axis_size("island")
    own_count = token_counts[0].astype(jnp.float32)
    total_count = lax.psum(own_count, "island")
    received = lax.all_to_all(
        own_count / total_count * delta, "island", split_axis=1, concat_axis=0, tiled=True
    )
    average = jnp.sum(received.reshape(groups, block, anchor.shape[1]), axis=0)
    new_momentum = outer_beta * outer_momentum + average
    new_anchor = anchor - outer_rate * (average + outer_beta * new_momentum)
    return (new_anchor, new_momentum)


MESH = pl.DeviceIdType.MESH
BF = jnp.bfloat16
F32 = jnp.float32


def dot(left, right):
    return jnp.dot(left, right, preferred_element_type=F32)


def round_kernel(
    ni,
    nf,
    hidden,
    query,
    keys_in,
    targets,
    segments,
    first_in,
    second_in,
    anchor_in,
    momentum_in,
    counts,
    new_anchor,
    new_momentum,
    q_buf,
    t_buf,
    keys,
    anchor,
    momentum,
    first,
    second,
    feat,
    feat_t,
    att,
    att_t,
    weight,
    master,
    delta,
    a_buf,
    c_buf,
    bv_send,
    bv_recv,
    vg_buf,
    d_send,
    d_recv,
    local_sem,
    h_send_sem,
    h_recv_sem,
    a_send_sem,
    a_recv_sem,
    c_send_sem,
    c_recv_sem,
    b_send_sem,
    b_recv_sem,
    v_send_sem,
    v_recv_sem,
    d_send_sem,
    d_recv_sem,
):
    me = lax.axis_index("fsdp")
    island = lax.axis_index("island")
    rows = feat.shape[1]
    block = feat.shape[2]
    columns = anchor.shape[0]
    group_rows = rows * nf
    scale_in = 1.0 / math.sqrt(hidden.shape[1])

    def ahead(step):
        return lax.rem(me + step, nf)

    def behind(step):
        return lax.rem(me + nf - step, nf)

    def peer(step):
        return lax.rem(island + step, ni)

    loads = [
        pltpu.make_async_copy(anchor_in, anchor, local_sem.at[0]),
        pltpu.make_async_copy(query, q_buf, local_sem.at[1]),
        pltpu.make_async_copy(targets, t_buf, local_sem.at[2]),
        pltpu.make_async_copy(first_in, first, local_sem.at[3]),
        pltpu.make_async_copy(second_in, second, local_sem.at[4]),
        pltpu.make_async_copy(keys_in, keys, local_sem.at[5]),
        pltpu.make_async_copy(momentum_in, momentum, local_sem.at[6]),
        pltpu.make_async_copy(
            hidden.at[:, pl.ds(pl.multiple_of(me * block, block), block)],
            feat.at[0],
            local_sem.at[7],
        ),
    ]
    for number in (0, 5, 1):
        loads[number].start()

    barrier = pltpu.get_barrier_semaphore()
    for step in range(1, nf):
        pl.semaphore_signal(
            barrier, inc=1, device_id=(island, ahead(step)), device_id_type=MESH
        )
    for step in range(1, ni):
        pl.semaphore_signal(barrier, inc=1, device_id=(peer(step), me), device_id_type=MESH)

    pl.semaphore_wait(barrier, ni + nf - 2)

    def send_hidden(step):
        return pltpu.make_async_remote_copy(
            src_ref=hidden.at[:, pl.ds(pl.multiple_of(ahead(step) * block, block), block)],
            dst_ref=feat.at[step],
            send_sem=h_send_sem.at[step],
            recv_sem=h_recv_sem.at[step],
            device_id=(island, ahead(step)),
            device_id_type=MESH,
        )

    def send_anchor(step):
        return pltpu.make_async_remote_copy(
            src_ref=a_buf.at[island],
            dst_ref=a_buf.at[island],
            send_sem=a_send_sem.at[step],
            recv_sem=a_recv_sem.at[island],
            device_id=(peer(step), me),
            device_id_type=MESH,
        )

    def await_anchor(step):
        owner = peer(step)
        return pltpu.make_async_remote_copy(
            src_ref=a_buf.at[owner],
            dst_ref=a_buf.at[owner],
            send_sem=a_send_sem.at[step],
            recv_sem=a_recv_sem.at[owner],
            device_id=(peer(step), me),
            device_id_type=MESH,
        )

    def send_count(step):
        return pltpu.make_async_remote_copy(
            src_ref=c_buf.at[island],
            dst_ref=c_buf.at[island],
            send_sem=c_send_sem.at[step],
            recv_sem=c_recv_sem.at[island],
            device_id=(peer(step), me),
            device_id_type=MESH,
        )

    def await_count(step):
        owner = peer(step)
        return pltpu.make_async_remote_copy(
            src_ref=c_buf.at[owner],
            dst_ref=c_buf.at[owner],
            send_sem=c_send_sem.at[step],
            recv_sem=c_recv_sem.at[owner],
            device_id=(owner, me),
            device_id_type=MESH,
        )

    def order(number):
        return lax.rem(number + island // 2, KVH)

    def send_block(turn, head, step):
        return pltpu.make_async_remote_copy(
            src_ref=bv_send.at[turn, head, step],
            dst_ref=bv_recv.at[turn, head, step],
            send_sem=b_send_sem.at[turn, head, step],
            recv_sem=b_recv_sem.at[turn, head, step],
            device_id=(island, behind(step)),
            device_id_type=MESH,
        )

    def send_grad(turn, head, step):
        return pltpu.make_async_remote_copy(
            src_ref=vg_buf.at[turn, head, 0:rows],
            dst_ref=vg_buf.at[turn, head, step * rows : (step + 1) * rows],
            send_sem=v_send_sem.at[turn, head, step],
            recv_sem=v_recv_sem.at[turn, head, step],
            device_id=(island, ahead(step)),
            device_id_type=MESH,
        )

    def send_delta(owner):
        return pltpu.make_async_remote_copy(
            src_ref=d_send.at[owner],
            dst_ref=d_recv.at[island],
            send_sem=d_send_sem.at[owner],
            recv_sem=d_recv_sem.at[island],
            device_id=(owner, me),
            device_id_type=MESH,
        )

    def await_delta(step):
        owner = peer(step)
        return pltpu.make_async_remote_copy(
            src_ref=d_send.at[owner],
            dst_ref=d_recv.at[owner],
            send_sem=d_send_sem.at[owner],
            recv_sem=d_recv_sem.at[owner],
            device_id=(owner, me),
            device_id_type=MESH,
        )

    near_first = [1, 3, 2] if nf == 4 else list(range(1, nf))
    far_first = [2, 1, 3] if nf == 4 else near_first
    for step in far_first:
        send_hidden(step).start()
    loads[0].wait()
    a_buf[island] = anchor[...].astype(BF)
    count = counts[0]
    high = (count // 256).astype(F32)
    low = (count % 256).astype(F32)
    upper = lax.broadcasted_iota(jnp.int32, (16, 128), 0) < 8
    c_buf[island] = jnp.where(upper, high, low).astype(BF)
    for step in range(1, ni):
        send_anchor(step).start()
        send_count(step).start()
    for number in (7, 2, 3, 4, 6):
        loads[number].start()

    loads[5].wait()
    loads[1].wait()
    seg = jnp.broadcast_to(segments[...].astype(F32), (rows, rows))
    place_t = lax.broadcasted_iota(jnp.int32, (rows, rows), 0)
    place_s = lax.broadcasted_iota(jnp.int32, (rows, rows), 1)
    allowed = (place_s <= place_t) & (seg == seg.T)

    def attend(number, carry):
        head = number // QPK
        within = number % QPK
        queries = q_buf[:, pl.ds(pl.multiple_of(number * HD, HD), HD)]
        keyed = keys[:, pl.ds(pl.multiple_of(head * HD, HD), HD)]
        scores = lax.dot_general(
            queries, keyed, (((1,), (1,)), ((), ())), preferred_element_type=F32
        ) * (1.0 / math.sqrt(HD))
        scores = jnp.where(allowed, scores, -1e30)
        expo = jnp.exp(scores - jnp.max(scores, axis=1, keepdims=True))
        ratio = expo / jnp.sum(expo, axis=1, keepdims=True)
        at = pl.ds(pl.multiple_of(within * rows, rows), rows)
        att[head, at, :] = ratio.astype(BF)
        att_t[head, :, at] = ratio.T.astype(BF)
        return carry

    lax.fori_loop(0, KVH * QPK, attend, 0, unroll=2)

    for step in range(1, ni):
        await_anchor(step).wait_recv()

    def merge(head, carry):
        both = jnp.concatenate([a_buf[2 * head], a_buf[2 * head + 1]], axis=0).T
        weight[head] = both
        master[head] = both.astype(F32)
        return carry

    lax.fori_loop(0, KVH, merge, 0)

    for step in [0] + near_first:
        if step == 0:
            loads[7].wait()
        else:
            send_hidden(step).wait_recv()

        def first_blocks(number, carry, step=step):
            head = order(number)
            piece = dot(feat[step], weight[head]).astype(BF)
            if step == 0:
                bv_recv[0, head, 0] = piece
            else:
                bv_send[0, head, step] = piece
                send_block(0, head, step).start()
            return carry

        lax.fori_loop(0, KVH, first_blocks, 0)
    for step in range(nf):
        feat_t[:, step * rows : (step + 1) * rows] = feat[step].T

    def attention_turn(turn, head):
        for step in range(1, nf):
            send_block(turn, head, step).wait_recv()
        projected = bv_recv[turn, head, 0].astype(F32)
        for step in range(1, nf):
            projected = projected + bv_recv[turn, head, step].astype(F32)
        values = (projected * scale_in).astype(BF)
        back = jnp.zeros((rows, HD), F32)
        for within in range(QPK):
            lot = slice(within * rows, (within + 1) * rows)
            mixed = dot(att[head, lot, :], values)
            aim = t_buf[:, pl.ds(pl.multiple_of((head * QPK + within) * HD, HD), HD)]
            error = ((mixed - aim.astype(F32)) * (1.0 / group_rows)).astype(BF)
            back = back + dot(att_t[head, :, lot], error)
        vg_buf[turn, head, 0:rows] = (back * scale_in).astype(BF)
        for step in far_first:
            send_grad(turn, head, step).start()

    def update_turn(turn, head):
        for step in range(1, nf):
            send_grad(turn, head, step).wait_recv()
        lanes = pl.ds(pl.multiple_of(head * HD, HD), HD)
        part = block // 4

        def rows_part(index, carry):
            at = pl.ds(pl.multiple_of(index * part, part), part)
            grad = dot(feat_t[at, :], vg_buf[turn, head])
            one = beta_one * first[0, at, lanes] + (1.0 - beta_one) * grad
            two = beta_two * second[0, at, lanes] + (1.0 - beta_two) * grad * grad
            now = master[head, at]
            move = inner_rate * (one / (jnp.sqrt(two) + epsilon) + decay * now)
            if turn == 0:
                first[0, at, lanes] = one
                second[0, at, lanes] = two
                delta[head, at] = move
                later = now - move
                master[head, at] = later
                weight[head, at] = later.astype(BF)
            else:
                delta[head, at] = (delta[head, at] + move) * count.astype(F32)
            return carry

        lax.fori_loop(0, 4, rows_part, 0)

    def turn_one_attention(number, carry):
        head = order(number)
        attention_turn(0, head)
        return carry

    def turn_one_update(number, carry):
        head = order(number)
        update_turn(0, head)
        for step in [1, 3, 2, 0] if nf == 4 else list(range(nf)):
            piece = dot(feat[step], weight[head]).astype(BF)
            if step == 0:
                bv_recv[1, head, 0] = piece
            else:
                bv_send[1, head, step] = piece
                send_block(1, head, step).start()
        return carry

    def turn_two_attention(number, carry):
        head = order(number)
        attention_turn(1, head)
        return carry

    def turn_two_update(number, carry):
        head = order(number)
        update_turn(1, head)
        turned = delta[head].astype(BF).T
        d_send[2 * head] = turned[:columns]
        d_send[2 * head + 1] = turned[columns:]
        for odd in range(2):
            owner = 2 * head + odd

            @pl.when(owner != island)
            def _():
                send_delta(owner).start()

        return carry

    loads[2].wait()
    lax.fori_loop(0, KVH, turn_one_attention, 0)
    loads[3].wait()
    loads[4].wait()
    turn_one_update(0, 0)

    def crossed(number, carry):
        turn_one_update(number, carry)
        turn_two_attention(number - 1, carry)
        return carry

    lax.fori_loop(1, KVH, crossed, 0)
    turn_two_update(0, 0)
    turn_two_attention(KVH - 1, 0)
    lax.fori_loop(1, KVH, turn_two_update, 0)

    for step in range(1, ni):
        await_delta(step).wait_recv()
    total = d_send[island].astype(F32)
    for step in range(1, ni):
        total = total + d_recv[peer(step)].astype(F32)
    tally = c_buf[island].astype(F32)
    for step in range(1, ni):
        await_count(step).wait_recv()
        tally = tally + c_buf[peer(step)].astype(F32)
    whole = tally[0:1, 0:1] * 256.0 + tally[8:9, 0:1]
    average = total / whole
    loads[6].wait()
    fresh = outer_beta * momentum[...] + average
    new_momentum[...] = fresh
    new_anchor[...] = anchor[...] - outer_rate * (average + outer_beta * fresh)

    for step in range(1, nf):
        send_hidden(step).wait_send()
    for step in range(1, ni):
        send_anchor(step).wait_send()
        send_count(step).wait_send()
        await_delta(step).wait_send()

    def drain(number, carry):
        turn = number // KVH
        head = number % KVH
        for step in range(1, nf):
            send_block(turn, head, step).wait_send()
            send_grad(turn, head, step).wait_send()
        return carry

    lax.fori_loop(0, 2 * KVH, drain, 0)


def on_device_any(*args):
    hidden, query, keys, _, _, first, _, anchor, _, _ = args
    ni = lax.axis_size("island")
    nf = lax.axis_size("fsdp")
    rows = hidden.shape[0]
    block, columns = anchor.shape
    if (rows, columns, ni, block) != (HD, HD // 2, 2 * KVH, 8 * HD):
        return on_device(*args)
    vmem = pl.BlockSpec(memory_space=pltpu.VMEM)
    anywhere = pl.BlockSpec(memory_space=pltpu.HBM)
    dma = pltpu.SemaphoreType.DMA
    args = args[:7] + (anchor.T, args[8].T, args[9])
    outs = pl.pallas_call(
        functools.partial(round_kernel, ni, nf),
        out_shape=[jax.ShapeDtypeStruct((columns, block), F32)] * 2,
        in_specs=[anywhere] * 4
        + [vmem]
        + [anywhere] * 4
        + [pl.BlockSpec(memory_space=pltpu.SMEM)],
        out_specs=[vmem, vmem],
        scratch_shapes=[
            pltpu.VMEM(query.shape, BF),
            pltpu.VMEM(query.shape, BF),
            pltpu.VMEM(keys.shape, BF),
            pltpu.VMEM((columns, block), F32),
            pltpu.VMEM((columns, block), F32),
            pltpu.VMEM(first.shape, F32),
            pltpu.VMEM(first.shape, F32),
            pltpu.VMEM((nf, rows, block), BF),
            pltpu.VMEM((block, nf * rows), BF),
            pltpu.VMEM((KVH, QPK * rows, rows), BF),
            pltpu.VMEM((KVH, rows, QPK * rows), BF),
            pltpu.VMEM((KVH, block, HD), BF),
            pltpu.VMEM((KVH, block, HD), F32),
            pltpu.VMEM((KVH, block, HD), F32),
            pltpu.VMEM((ni, columns, block), BF),
            pltpu.VMEM((ni, 16, 128), BF),
            pltpu.VMEM((2, KVH, nf, rows, HD), BF),
            pltpu.VMEM((2, KVH, nf, rows, HD), BF),
            pltpu.VMEM((2, KVH, nf * rows, HD), BF),
            pltpu.VMEM((ni, columns, block), BF),
            pltpu.VMEM((ni, columns, block), BF),
            dma((8,)),
            dma((nf,)),
            dma((nf,)),
            dma((ni,)),
            dma((ni,)),
            dma((ni,)),
            dma((ni,)),
            dma((2, KVH, nf)),
            dma((2, KVH, nf)),
            dma((2, KVH, nf)),
            dma((2, KVH, nf)),
            dma((ni,)),
            dma((ni,)),
        ],
        compiler_params=pltpu.CompilerParams(
            collective_id=0, has_side_effects=True, vmem_limit_bytes=62 * 2**20
        ),
    )(*args)
    return tuple(out.T for out in outs)


def solution(mesh):
    in_specs = (
        P(("island", "fsdp"), None),
        P(("island", "fsdp"), None),
        P(("island", "fsdp"), None),
        P(("island", "fsdp"), None),
        P(("island", "fsdp"), None),
        P("island", "fsdp", None),
        P("island", "fsdp", None),
        P("fsdp", "island"),
        P("fsdp", "island"),
        P("island"),
    )
    out_specs = (P("fsdp", "island"), P("fsdp", "island"))
    return jax.shard_map(
        on_device_any, mesh=mesh, in_specs=in_specs, out_specs=out_specs, check_vma=False
    )
```
